32 devices in a mesh: inst: 16 (over z, x, core), tp: 2 (over y).
Axes of the slice: x: 2, y: 2, z: 4, core: 2. Of those that a mesh axis runs over, the one named last changes fastest.
Arguments:
- step_queries: bfloat16 [4, 128, 8192], P(None, 'inst', 'tp'), may hold values from -11 to 11
- step_keyvals: bfloat16 [4, 128, 8, 256], P(None, 'inst', 'tp'), may hold values from -9.5 to 9.5
- cache_pages: bfloat16 [2048, 16, 8, 256], P('inst', None, 'tp'), may hold values from -9.5 to 9.5
- block_table: int32 [128, 16], P('inst'), may hold values from 0 to 127, as said below
- context_len: int32 [128], replicated, may hold values from 1 to 256, as said below
- partner: int32 [16], replicated, may hold values from 0 to 15, as said below
- moved_slot: int32 [16], replicated, may hold values from 0 to 7
- prompt_queries: bfloat16 [2048, 8192], P(('inst', 'tp')), may hold values from -11 to 11
- prompt_keyvals: bfloat16 [2048, 8, 256], P(('inst', 'tp')), may hold values from -9.5 to 9.5
- prompt_target: int32 [2048, 1], replicated, may hold values from 0 to 15; in each aligned block of 64 rows (0 to 63, 64 to 127, ...) at most 8 rows name the same one
Outputs:
- decode_output: bfloat16 [4, 128, 8192], P(None, 'inst', 'tp')
- prefill_output: bfloat16 [4096, 8192], P('inst', 'tp')
The draws below stay inside these ranges and needn't reach their ends.
Inputs may be any that keep to these rules, and one draw needn't show every extreme that they name: partner[partner[i]] = i, and i and partner[i] differ in exactly one bit. `block_table`: the 8 rows of one instance together name each of its 128 pages once. `context_len`: some request holds exactly 256 tokens. `prompt_target`: among the 64 rows of one device no instance is named more than 8 times.
All inputs are finite; a program needn't handle non-finite values.
Results may differ from the reference program's by a relative error of at most 0.0049.
Values may be sent and summed in bfloat16 or wider, within the bound.
A program may use at most 64 MiB of HBM per device.

```python
import math
import jax
import jax.numpy as jnp
import numpy as np
from jax import lax

H = 64
KVH = 8
HD = 128
REQ = 8
PAGE = 16
MAXP = 16
STEPS = 4
ROWS_DEV = 64
CTX = 256
POOL = 128
CAP = 8
SLOTS = 256
ROWS = 2048
N_INST = 16
N_TP = 2


def keyval_law(key, shape):
    drawn = jnp.clip(jax.random.normal(key, shape, jnp.float32), -6.0, 6.0)
    return drawn.astype(jnp.bfloat16)


def query_law(key, shape):
    drawn = jnp.clip(jax.random.normal(key, shape, jnp.float32), -6.0, 6.0)
    return drawn.astype(jnp.bfloat16)


def draw_step_queries(key, part):
    return query_law(jax.random.fold_in(key, 21), (STEPS, N_INST * REQ, H * HD))


def draw_step_keyvals(key, part):
    return keyval_law(jax.random.fold_in(key, 22), (STEPS, N_INST * REQ, KVH, 2 * HD))


def draw_cache_pages(key, part):
    return keyval_law(jax.random.fold_in(key, 23), (N_INST * POOL, PAGE, KVH, 2 * HD))


def draw_prompt_queries(key, part):
    return query_law(jax.random.fold_in(key, 24), (ROWS, H * HD))


def draw_prompt_keyvals(key, part):
    return keyval_law(jax.random.fold_in(key, 25), (ROWS, KVH, 2 * HD))


def shuffled_pool(key):
    return jax.random.permutation(key, POOL).astype(jnp.int32)


def draw_block_table(key, part):
    keys = jax.random.split(jax.random.fold_in(key, 31), N_INST)
    tables = jax.vmap(shuffled_pool)(keys)
    return tables.reshape(N_INST * REQ, MAXP).astype(jnp.int32)


def draw_context_len(key, part):
    base = jax.random.fold_in(key, 41)
    lengths = jax.random.randint(base, (N_INST * REQ,), 1, CTX + 1, dtype=jnp.int32)
    spot = jax.random.randint(jax.random.fold_in(base, 1), (), 0, N_INST * REQ, dtype=jnp.int32)
    return lengths.at[spot].set(CTX).astype(jnp.int32)


def draw_partner(key, part):
    base = jax.random.fold_in(key, 51)
    width = N_INST.bit_length() - 1
    index = jnp.arange(N_INST, dtype=jnp.int32)
    order = jax.random.permutation(jax.random.fold_in(base, 1), width).astype(jnp.int32)
    flags = jax.random.randint(jax.random.fold_in(base, 2), (width, N_INST), 0, 2, dtype=jnp.int32)
    chosen = jnp.full((N_INST,), -1, dtype=jnp.int32)
    for level in range(width):
        cube = jnp.zeros((N_INST,), dtype=jnp.int32)
        for lower in range(level):
            digit = jnp.bitwise_and(jnp.right_shift(index, order[lower]), 1)
            cube = cube + jnp.left_shift(digit, lower)
        flag = flags[level][cube]
        if level == width - 1:
            flag = jnp.ones_like(flag)
        chosen = jnp.where((chosen < 0) & (flag > 0), order[level], chosen)
    return jnp.bitwise_xor(index, jnp.left_shift(jnp.int32(1), chosen)).astype(jnp.int32)


def place_ends(drawn, stream_key, smallest, high):
    index_at = [jax.random.randint(jax.random.fold_in(stream_key, axis), (), 0, length) for axis, length in enumerate(drawn.shape)]
    longest = drawn.shape.index(max(drawn.shape))
    neighbour = index_at[:longest] + [(index_at[longest] + 1) % drawn.shape[longest]] + index_at[longest + 1:]
    return drawn.at[tuple(index_at)].set(smallest).at[tuple(neighbour)].set(high)


def deal_out(own_key, own, number, rows, number_of, top, bound, lean):
    order = jax.random.permutation(own_key, number_of)
    packed, ordinary = load_shares(number_of, rows * top, bound, lean, True), load_shares(number_of, rows * top, bound, lean, False)
    places = jnp.arange(number_of)

    def named(sizes, rotation):
        used = int((sizes > 0).sum())
        fixed = max(1, used // 4)
        moved = fixed + (places - fixed + rotation * (used - fixed)) % max(1, number_of - fixed)
        return jnp.zeros((number_of,), jnp.int32).at[order[jnp.where(places < fixed, places, moved)]].set(jnp.asarray(sizes, jnp.int32))

    sizes = jnp.where(number % 4 == 0, named(packed, number // 4), named(ordinary, number - number // 4 - 1))
    mixed = jax.random.permutation(jax.random.fold_in(own, 3), number_of)
    source_of, receiver = mixed[0:number_of // 2 * 2:2], mixed[1:number_of // 2 * 2:2]
    margin = jnp.minimum(sizes[source_of] - 1, bound - sizes[receiver]) // 2
    margin = jnp.where((source_of == order[0]) | (receiver == order[0]) | (sizes[receiver] == 0), 0, jnp.maximum(margin, 0))
    moved = jax.random.randint(jax.random.fold_in(own, 4), (number_of // 2,), 0, 1 << 20) % (margin + 1)
    sizes = sizes.at[source_of].add(-moved).at[receiver].add(moved)
    members = jnp.searchsorted(jnp.cumsum(sizes), jnp.arange(rows * top), side="right").astype(jnp.int32)
    listing = members.reshape(top, rows).T
    listing = listing[jax.random.permutation(jax.random.fold_in(own, 1), rows)]
    rotation = jax.random.randint(jax.random.fold_in(own, 2), (rows, 1), 0, top)
    return jnp.take_along_axis(listing, (jnp.arange(top)[None, :] + rotation) % top, axis=1)


def load_shares(number_of, total, most, slope, full):
    loads = [(1 << 20) // math.isqrt(standing ** slope) + 1 for standing in range(1, number_of + 1)]
    largest = most if full else min(most, max(-(-total // number_of), total * loads[0] // sum(loads)))
    least = 1 if total - largest >= number_of - 1 else 0
    given, rest = [largest] + [least] * (number_of - 1), total - largest - least * (number_of - 1)
    while rest > 0:
        movable = [i for i in range(1, number_of) if given[i] < largest] or [i for i in range(1, number_of) if given[i] < most]
        pool, budget = sum([loads[i] for i in movable]), rest
        for i in movable:
            extra = min(most - given[i], max(1, budget * loads[i] // pool), rest)
            given[i] = given[i] + extra
            rest = rest - extra
    return np.array(given)


def setup_inputs(seed: int = 0) -> dict:
    seeds = jax.random.split(jax.random.key(seed), 11)
    step_queries = draw_step_queries(jax.random.fold_in(seeds[10], 71), 0)
    step_keyvals = draw_step_keyvals(jax.random.fold_in(seeds[10], 71), 0)
    cache_pages = draw_cache_pages(jax.random.fold_in(seeds[10], 71), 0)
    block_table = draw_block_table(jax.random.fold_in(seeds[10], 71), 0)
    context_len = draw_context_len(jax.random.fold_in(seeds[10], 71), 0)
    partner = draw_partner(jax.random.fold_in(seeds[10], 71), 0)
    moved_slot = place_ends(jax.random.randint(seeds[6], (N_INST,), 0, REQ), jax.random.fold_in(seeds[6], 1), 0, REQ - 1).astype(jnp.int32)
    prompt_queries = draw_prompt_queries(jax.random.fold_in(seeds[10], 71), 0)
    prompt_keyvals = draw_prompt_keyvals(jax.random.fold_in(seeds[10], 71), 0)
    prompt_target_keys = jax.random.split(jax.random.fold_in(seeds[9], 1), ROWS // ROWS_DEV)
    prompt_target_turns = jax.random.permutation(jax.random.fold_in(seeds[9], 3), ROWS // ROWS_DEV)
    prompt_target = jax.vmap(lambda own, number: deal_out(jax.random.fold_in(seeds[9], 2), own, number, ROWS_DEV, N_INST, 1, CAP, 2))(prompt_target_keys, prompt_target_turns).reshape((ROWS, 1))
    return {"step_queries": step_queries, "step_keyvals": step_keyvals, "cache_pages": cache_pages, "block_table": block_table, "context_len": context_len, "partner": partner, "moved_slot": moved_slot, "prompt_queries": prompt_queries, "prompt_keyvals": prompt_keyvals, "prompt_target": prompt_target}


def masked_weights(scores, mask):
    shifted = jnp.where(mask, scores, jnp.float32(-1e30))
    top = jnp.max(shifted, axis=-1, keepdims=True)
    expo = jnp.where(mask, jnp.exp(shifted - top), jnp.float32(0.0))
    total = jnp.sum(expo, axis=-1, keepdims=True)
    total = jnp.where(total > 0, total, jnp.float32(1.0))
    return expo / total


def round_weights(weights):
    rounded = lax.optimization_barrier(weights.astype(jnp.bfloat16))
    return rounded.astype(jnp.float32)


def decode_part(step_queries, step_keyvals, cache_pages, block_table, context_len, partner, moved_slot):
    group = H // KVH
    scale = HD ** -0.5
    inst = jnp.arange(N_INST, dtype=jnp.int32)
    slot = jnp.arange(REQ, dtype=jnp.int32)
    moved = slot[None, :] == moved_slot[:, None]
    src_inst = jnp.where(moved, partner[:, None], inst[:, None]).astype(jnp.int32)
    src_slot = jnp.where(moved, moved_slot[partner][:, None], slot[None, :]).astype(jnp.int32)
    source = (src_inst * REQ + src_slot).reshape(-1).astype(jnp.int32)
    pages = (block_table[source] + (src_inst.reshape(-1) * POOL)[:, None]).astype(jnp.int32)
    lengths = context_len[source]

    def one_request(items):
        queries, fresh, page_ids, length = items
        context = cache_pages[page_ids].reshape(CTX, KVH, 2 * HD).astype(jnp.float32)
        fresh = fresh.astype(jnp.float32)
        query = queries.astype(jnp.float32).reshape(STEPS, KVH, group, HD)
        past = jnp.einsum('tkgd,ckd->tkgc', query, context[:, :, :HD]) * scale
        newer = jnp.einsum('tkgd,ukd->tkgu', query, fresh[:, :, :HD]) * scale
        past_mask = jnp.broadcast_to((jnp.arange(CTX, dtype=jnp.int32) < length)[None, None, None, :], past.shape)
        step_ids = jnp.arange(STEPS, dtype=jnp.int32)
        new_mask = jnp.broadcast_to((step_ids[None, :] <= step_ids[:, None])[:, None, None, :], newer.shape)
        weights = masked_weights(jnp.concatenate([past, newer], axis=-1), jnp.concatenate([past_mask, new_mask], axis=-1))
        weights = round_weights(weights)
        out = jnp.einsum('tkgc,ckd->tkgd', weights[..., :CTX], context[:, :, HD:])
        out = out + jnp.einsum('tkgu,ukd->tkgd', weights[..., CTX:], fresh[:, :, HD:])
        return out.reshape(STEPS, H * HD).astype(jnp.bfloat16)

    decoded = lax.map(one_request, (jnp.transpose(step_queries, (1, 0, 2)), jnp.transpose(step_keyvals, (1, 0, 2, 3)), pages, lengths))
    return jnp.transpose(decoded, (1, 0, 2))


def prefill_part(prompt_queries, prompt_keyvals, prompt_target):
    group = H // KVH
    scale = HD ** -0.5
    devices = N_INST * N_TP
    target = prompt_target[:, 0].reshape(devices, ROWS_DEV).astype(jnp.int32)
    onehot = (target[:, :, None] == jnp.arange(N_INST, dtype=jnp.int32)[None, None, :]).astype(jnp.int32)
    before = (jnp.cumsum(onehot, axis=1) - onehot).astype(jnp.int32)
    rank = jnp.sum(before * onehot, axis=2).astype(jnp.int32)
    slot = (jnp.arange(devices, dtype=jnp.int32)[:, None] * CAP + rank).astype(jnp.int32)
    table = jnp.full((N_INST, SLOTS), -1, dtype=jnp.int32)
    table = table.at[target.reshape(-1), slot.reshape(-1)].set(jnp.arange(ROWS, dtype=jnp.int32))
    positions = jnp.arange(SLOTS, dtype=jnp.int32)

    def one_instance(row_ids):
        valid = row_ids >= 0
        safe = jnp.maximum(row_ids, 0).astype(jnp.int32)
        query = prompt_queries[safe].astype(jnp.float32).reshape(SLOTS, KVH, group, HD)
        keyval = prompt_keyvals[safe].astype(jnp.float32)
        mask = (valid[None, :] & (positions[None, :] <= positions[:, None]))[None]

        def one_head(items):
            head_query, head_keyval = items
            scores = jnp.einsum('qgd,cd->gqc', head_query, head_keyval[:, :HD]) * scale
            weights = round_weights(masked_weights(scores, jnp.broadcast_to(mask, scores.shape)))
            return jnp.einsum('gqc,cd->qgd', weights, head_keyval[:, HD:])

        outs = lax.map(one_head, (jnp.transpose(query, (1, 0, 2, 3)), jnp.transpose(keyval, (1, 0, 2))))
        outs = jnp.transpose(outs, (1, 0, 2, 3)).reshape(SLOTS, H * HD)
        return jnp.where(valid[:, None], outs, jnp.float32(0.0)).astype(jnp.bfloat16)

    return lax.map(one_instance, table).reshape(N_INST * SLOTS, H * HD)


def reference(step_queries, step_keyvals, cache_pages, block_table, context_len, partner, moved_slot, prompt_queries, prompt_keyvals, prompt_target):
    decode_output = decode_part(step_queries, step_keyvals, cache_pages, block_table, context_len, partner, moved_slot)
    prefill_output = prefill_part(prompt_queries, prompt_keyvals, prompt_target)
    return (decode_output, prefill_output)
```

```python
import functools
import math

import jax
import jax.numpy as jnp
from jax import lax
from jax.experimental import pallas as pl
from jax.experimental.pallas import tpu as pltpu
from jax.sharding import PartitionSpec as P


def swapped(array, axis, bit):
    return lax.ppermute(array, axis, [(i, i ^ 1 << bit) for i in range(lax.axis_size(axis))])


def masked_weights(scores, mask):
    shifted = jnp.where(mask, scores, jnp.float32(-1e30))
    top = jnp.max(shifted, axis=-1, keepdims=True)
    expo = jnp.where(mask, jnp.exp(shifted - top), jnp.float32(0.0))
    total = jnp.sum(expo, axis=-1, keepdims=True)
    total = jnp.where(total > 0, total, jnp.float32(1.0))
    return expo / total


def decode_block(queries, context, lengths, fresh):
    steps, count, width = queries.shape
    kv_heads = context.shape[2]
    head_dim = context.shape[3] // 2
    group = width // (kv_heads * head_dim)
    span = context.shape[1]
    scale = head_dim ** (-0.5)
    query = queries.reshape(steps, count, kv_heads, group, head_dim)
    past = (
        jnp.einsum(
            "trkgd,rckd->trkgc", query, context[..., :head_dim], preferred_element_type=jnp.float32
        )
        * scale
    )
    newer = (
        jnp.einsum(
            "trkgd,urkd->trkgu", query, fresh[..., :head_dim], preferred_element_type=jnp.float32
        )
        * scale
    )
    past_mask = (jnp.arange(span, dtype=jnp.int32)[None, :] < lengths[:, None])[
        None, :, None, None, :
    ]
    step_ids = jnp.arange(steps, dtype=jnp.int32)
    new_mask = (step_ids[None, :] <= step_ids[:, None])[:, None, None, None, :]
    mask = jnp.concatenate(
        [jnp.broadcast_to(past_mask, past.shape), jnp.broadcast_to(new_mask, newer.shape)], axis=-1
    )
    weights = masked_weights(jnp.concatenate([past, newer], axis=-1), mask).astype(jnp.bfloat16)
    out = jnp.einsum(
        "trkgc,rckd->trkgd",
        weights[..., :span],
        context[..., head_dim:],
        preferred_element_type=jnp.float32,
    )
    out = out + jnp.einsum(
        "trkgu,urkd->trkgd",
        weights[..., span:],
        fresh[..., head_dim:],
        preferred_element_type=jnp.float32,
    )
    return out.reshape(steps, count, width).astype(jnp.bfloat16)


def prefill_block(queries, keyvals, valid):
    slots, width = queries.shape
    kv_heads = keyvals.shape[1]
    head_dim = keyvals.shape[2] // 2
    group = width // (kv_heads * head_dim)
    scale = head_dim ** (-0.5)
    query = queries.reshape(slots, kv_heads, group, head_dim)
    block = 512 if slots % 512 == 0 else slots
    pieces = []
    for start in range(0, slots, block):
        finish = start + block
        scores = (
            jnp.einsum(
                "qkgd,ckd->kgqc",
                query[start:finish],
                keyvals[:finish, :, :head_dim],
                preferred_element_type=jnp.float32,
            )
            * scale
        )
        query_pos = jnp.arange(start, finish, dtype=jnp.int32)
        key_pos = jnp.arange(finish, dtype=jnp.int32)
        mask = (valid[None, :finish] & (key_pos[None, :] <= query_pos[:, None]))[None, None]
        weights = masked_weights(scores, jnp.broadcast_to(mask, scores.shape)).astype(jnp.bfloat16)
        out = jnp.einsum(
            "kgqc,ckd->qkgd",
            weights,
            keyvals[:finish, :, head_dim:],
            preferred_element_type=jnp.float32,
        )
        out = jnp.where(valid[start:finish, None, None, None], out, jnp.float32(0.0))
        pieces.append(out.reshape(block, width).astype(jnp.bfloat16))
    return jnp.concatenate(pieces, axis=0)


MESH = pl.DeviceIdType.MESH
NEG = -1e30


def fused_kernel(
    n_inst,
    n_tp,
    block_ref,
    length_ref,
    partner_ref,
    moved_ref,
    step_q_ref,
    step_kv_ref,
    cache_hbm,
    prompt_q_ref,
    prompt_kv_ref,
    target_ref,
    decode_ref,
    prefill_ref,
    cache_ref,
    send_ref,
    recv_ref,
    step_ref,
    context_ref,
    decoded_ref,
    move_q_out,
    move_kv_out,
    move_q_in,
    move_kv_in,
    move_o_out,
    move_o_in,
    bias_ref,
    cache_sem,
    self_sem,
    send_sem,
    recv_sem,
    move_send_sem,
    move_recv_sem,
):
    f32, bf16 = jnp.float32, jnp.bfloat16
    me_inst, me_tp = lax.axis_index("inst"), lax.axis_index("tp")
    me = me_inst * n_tp + me_tp
    devices = n_inst * n_tp
    bits = n_inst.bit_length() - 1
    steps, requests, width = step_q_ref.shape
    kv_heads, both = step_kv_ref.shape[2:]
    head = both // 2
    heads = width // head
    group = heads // kv_heads
    rows = prompt_q_ref.shape[0]
    cap = recv_ref.shape[1]
    slots = devices * cap
    pages, page = block_ref.shape[1], cache_ref.shape[1]
    unit = group * head + both
    factor = head**-0.5 * math.log2(math.e)

    cache_copy = pltpu.make_async_copy(cache_hbm, cache_ref, cache_sem)
    cache_copy.start()

    barrier = pltpu.get_barrier_semaphore()
    for turn in range(1, devices):
        inst = lax.rem(me_inst + turn // n_tp, n_inst)
        tp = lax.rem(me_tp + turn % n_tp, n_tp)
        pl.semaphore_signal(barrier, inc=1, device_id=(inst, tp), device_id_type=MESH)

    for t in range(steps):
        for h in range(heads):
            step_ref[t * heads + h] = step_q_ref[t, :, h * head : (h + 1) * head].astype(f32)
    my_slot = moved_ref[me_inst]
    distance = partner_ref[me_inst] - me_inst
    move_q_out[...] = step_ref[:, my_slot, :].astype(bf16)
    move_kv_out[...] = step_kv_ref[:, my_slot].reshape(steps * kv_heads, both)

    mine = target_ref[pl.ds(pl.multiple_of(me * rows, rows), rows), :].astype(f32)
    onehot = (
        mine == lax.broadcasted_iota(jnp.int32, (rows, n_inst), 1).astype(f32)
    ).astype(f32)
    earlier = (
        lax.broadcasted_iota(jnp.int32, (rows, rows), 1)
        < lax.broadcasted_iota(jnp.int32, (rows, rows), 0)
    ).astype(bf16)
    before = jnp.dot(earlier, onehot.astype(bf16), preferred_element_type=f32)
    rank = jnp.sum(before * onehot, axis=1, keepdims=True)
    place = mine * cap + rank
    dispatch = (
        lax.broadcasted_iota(jnp.int32, (rows, n_inst * cap), 1).astype(f32) == place
    ).astype(f32)
    dispatch = jnp.transpose(dispatch).astype(bf16)

    def pack(tp):
        for h in range(kv_heads):
            start = (tp * kv_heads + h) * group * head
            queries = prompt_q_ref[:, start : start + group * head]
            packed = jnp.dot(dispatch, queries, preferred_element_type=f32)
            send_ref[tp, :, :, h * unit : h * unit + group * head] = packed.reshape(
                n_inst, cap, group * head
            ).astype(bf16)
            keyvals = prompt_kv_ref[:, tp * kv_heads + h, :]
            packed = jnp.dot(dispatch, keyvals, preferred_element_type=f32)
            send_ref[tp, :, :, h * unit + group * head : (h + 1) * unit] = packed.reshape(
                n_inst, cap, both
            ).astype(bf16)

    for tp in range(n_tp):
        pack(tp)

    def neighbour(bit):
        return me_inst + (1 - 2 * lax.rem(me_inst // (1 << bit), 2)) * (1 << bit)

    def move(bit, source, target, which):
        return pltpu.make_async_remote_copy(
            src_ref=source,
            dst_ref=target.at[bit],
            send_sem=move_send_sem.at[which, bit],
            recv_sem=move_recv_sem.at[which, bit],
            device_id=(neighbour(bit), me_tp),
            device_id_type=MESH,
        )

    pl.semaphore_wait(barrier, devices - 1)
    moves = []
    for bit in range(bits):
        moves.append(move(bit, move_q_out, move_q_in, 0))
        moves.append(move(bit, move_kv_out, move_kv_in, 1))
    for copy in moves:
        copy.start()

    own = pltpu.make_async_copy(send_ref.at[me_tp, me_inst], recv_ref.at[me], self_sem)
    own.start()
    copies = []
    order = []
    half = n_inst // 2
    for k in range(half):
        order.extend([half + k, k])
    for k in order:
        for t in range(n_tp):
            if k == 0 and t == 0:
                continue
            inst, tp = lax.rem(me_inst + k, n_inst), lax.rem(me_tp + t, n_tp)
            back_inst = lax.rem(me_inst + n_inst - k, n_inst)
            back_tp = lax.rem(me_tp + n_tp - t, n_tp)
            copy = pltpu.make_async_remote_copy(
                src_ref=send_ref.at[tp, inst],
                dst_ref=recv_ref.at[me],
                send_sem=send_sem.at[k * n_tp + t],
                recv_sem=recv_sem.at[k * n_tp + t],
                device_id=(inst, tp),
                device_id_type=MESH,
            )
            copy.start()
            arrival = pltpu.make_async_remote_copy(
                src_ref=send_ref.at[tp, inst],
                dst_ref=recv_ref.at[back_inst * n_tp + back_tp],
                send_sem=send_sem.at[k * n_tp + t],
                recv_sem=recv_sem.at[k * n_tp + t],
                device_id=(inst, tp),
                device_id_type=MESH,
            )
            copies.append((copy, arrival))

    here = (target_ref[...] == me_inst).astype(f32).reshape(devices, rows, 1)
    counts = jnp.sum(here, axis=1, keepdims=True)
    ranks = lax.broadcasted_iota(jnp.int32, (devices, cap, 1), 1).astype(f32)
    filled = (ranks < counts).astype(f32).reshape(slots, 1)
    across = jnp.transpose(jnp.broadcast_to(filled, (slots, 128)))[0:1, :]
    query_pos = lax.broadcasted_iota(jnp.int32, (slots, slots), 0)
    key_pos = lax.broadcasted_iota(jnp.int32, (slots, slots), 1)
    bias_ref[...] = jnp.where((key_pos <= query_pos) & (across > 0), 0.0, NEG)

    cache_copy.wait()
    for copy in moves:
        copy.wait()
    moved_q, moved_kv = move_q_in[0].astype(f32), move_kv_in[0].astype(f32)
    for bit in range(1, bits):
        match = (distance == (1 << bit)) | (distance == -(1 << bit))
        moved_q = jnp.where(match, move_q_in[bit].astype(f32), moved_q)
        moved_kv = jnp.where(match, move_kv_in[bit].astype(f32), moved_kv)
    moved_q, moved_kv = moved_q.astype(bf16), moved_kv.astype(bf16)

    queries_all = steps * heads
    span = pages * page * kv_heads
    fresh_all = steps * kv_heads
    query_row = lax.broadcasted_iota(jnp.int32, (queries_all, 1), 0)
    query_head = lax.rem(query_row, heads) // group
    query_step = query_row // heads
    past_col = lax.broadcasted_iota(jnp.int32, (1, span), 1)
    past_head, past_token = lax.rem(past_col, kv_heads), past_col // kv_heads
    fresh_col = lax.broadcasted_iota(jnp.int32, (1, fresh_all), 1)
    fresh_mask = (lax.rem(fresh_col, kv_heads) == query_head) & (
        fresh_col // kv_heads <= query_step
    )
    contract = (((1,), (1,)), ((), ()))

    def decode_slot(slot, carry):
        for i in range(pages):
            context_ref[i * page * kv_heads : (i + 1) * page * kv_heads, :] = cache_ref[
                block_ref[slot, i]
            ].reshape(page * kv_heads, both)
        is_moved = slot == my_slot
        queries = jnp.where(is_moved, moved_q, step_ref[:, slot, :].astype(bf16))
        fresh = jnp.where(
            is_moved, moved_kv, step_kv_ref[:, slot].reshape(fresh_all, both)
        )
        length = length_ref[me_inst * requests + slot]
        past = lax.dot_general(
            queries, context_ref[:, :head], contract, preferred_element_type=f32
        )
        newer = lax.dot_general(queries, fresh[:, :head], contract, preferred_element_type=f32)
        past = jnp.where((past_head == query_head) & (past_token < length), past, NEG)
        newer = jnp.where(fresh_mask, newer, NEG)
        top = jnp.maximum(
            jnp.max(past, axis=1, keepdims=True), jnp.max(newer, axis=1, keepdims=True)
        )
        past = jnp.exp2((past - top) * factor)
        newer = jnp.exp2((newer - top) * factor)
        total = jnp.sum(past, axis=1, keepdims=True) + jnp.sum(newer, axis=1, keepdims=True)
        share = 1.0 / total
        out = jnp.dot(
            (past * share).astype(bf16), context_ref[:, head:], preferred_element_type=f32
        )
        out = out + jnp.dot(
            (newer * share).astype(bf16), fresh[:, head:], preferred_element_type=f32
        )
        decoded_ref[:, slot, :] = out
        return carry

    lax.fori_loop(0, requests, decode_slot, 0)

    move_o_out[...] = decoded_ref[:, my_slot, :].astype(bf16)
    returns = [move(bit, move_o_out, move_o_in, 2) for bit in range(bits)]
    for copy in returns:
        copy.start()
    for copy in returns:
        copy.wait()
    moved_o = move_o_in[0].astype(f32)
    for bit in range(1, bits):
        match = (distance == (1 << bit)) | (distance == -(1 << bit))
        moved_o = jnp.where(match, move_o_in[bit].astype(f32), moved_o)
    slot_row = lax.broadcasted_iota(jnp.int32, (requests, 1), 0)
    for t in range(steps):
        for h in range(heads):
            row = t * heads + h
            decode_ref[t, :, h * head : (h + 1) * head] = jnp.where(
                slot_row == my_slot, moved_o[row : row + 1, :], decoded_ref[row]
            ).astype(bf16)

    own.wait()
    for copy, arrival in copies:
        copy.wait_send()
        arrival.wait_recv()

    def prefill_head(h, carry):
        base = pl.multiple_of(h * unit, 128)
        keyvals = (
            recv_ref[:, :, pl.ds(pl.multiple_of(base + group * head, 128), both)]
            .astype(f32)
            .reshape(slots, both)
            .astype(bf16)
        )
        keys = keyvals[:, :head]
        values = jnp.concatenate([keyvals[:, head:], jnp.ones((slots, head), bf16)], axis=1)
        for g in range(group):
            queries = (
                recv_ref[:, :, pl.ds(pl.multiple_of(base + g * head, 128), head)]
                .astype(f32)
                .reshape(slots, head)
                .astype(bf16)
            )
            for first in (0, slots // 2):
                last = first + slots // 2
                scores = lax.dot_general(
                    queries[first:last], keys[:last], contract, preferred_element_type=f32
                )
                scores = scores + bias_ref[first:last, :last]
                top = jnp.max(scores, axis=1, keepdims=True)
                expo = jnp.exp2((scores - top) * factor).astype(bf16)
                out = jnp.dot(expo, values[:last], preferred_element_type=f32)
                out = out[:, :head] / out[:, head:]
                out = jnp.where(filled[first:last] > 0, out, 0.0)
                prefill_ref[
                    first:last, pl.ds(pl.multiple_of((h * group + g) * head, 128), head)
                ] = out.astype(bf16)
        return carry

    lax.fori_loop(0, kv_heads, prefill_head, 0)


def local_fused(
    step_queries,
    step_keyvals,
    cache_pages,
    block_table,
    context_len,
    partner,
    moved_slot,
    prompt_queries,
    prompt_keyvals,
    prompt_target,
):
    n_inst, n_tp = lax.axis_size("inst"), lax.axis_size("tp")
    devices = n_inst * n_tp
    bits = n_inst.bit_length() - 1
    steps, requests, width = step_queries.shape
    kv_heads, both = step_keyvals.shape[2:]
    head = both // 2
    heads = width // head
    cap = 2 * prompt_queries.shape[0] // n_inst
    slots = devices * cap
    columns = width + kv_heads * both
    span = block_table.shape[1] * cache_pages.shape[1] * kv_heads
    bf16, f32 = jnp.bfloat16, jnp.float32
    smem = pl.BlockSpec(memory_space=pltpu.SMEM)
    vmem = pl.BlockSpec(memory_space=pltpu.VMEM)
    return pl.pallas_call(
        functools.partial(fused_kernel, n_inst, n_tp),
        out_shape=(
            jax.ShapeDtypeStruct(step_queries.shape, bf16),
            jax.ShapeDtypeStruct((slots, width), bf16),
        ),
        in_specs=[smem] * 4
        + [vmem, vmem, pl.BlockSpec(memory_space=pl.ANY), vmem, vmem, vmem],
        out_specs=(vmem, vmem),
        scratch_shapes=[
            pltpu.VMEM(cache_pages.shape, bf16),
            pltpu.VMEM((n_tp, n_inst, cap, columns), bf16),
            pltpu.VMEM((devices, cap, columns), bf16),
            pltpu.VMEM((steps * heads, requests, head), f32),
            pltpu.VMEM((span, both), bf16),
            pltpu.VMEM((steps * heads, requests, head), f32),
            pltpu.VMEM((steps * heads, head), bf16),
            pltpu.VMEM((steps * kv_heads, both), bf16),
            pltpu.VMEM((bits, steps * heads, head), bf16),
            pltpu.VMEM((bits, steps * kv_heads, both), bf16),
            pltpu.VMEM((steps * heads, head), bf16),
            pltpu.VMEM((bits, steps * heads, head), bf16),
            pltpu.VMEM((slots, slots), f32),
            pltpu.SemaphoreType.DMA,
            pltpu.SemaphoreType.DMA,
            pltpu.SemaphoreType.DMA((devices,)),
            pltpu.SemaphoreType.DMA((devices,)),
            pltpu.SemaphoreType.DMA((3, bits)),
            pltpu.SemaphoreType.DMA((3, bits)),
        ],
        compiler_params=pltpu.CompilerParams(
            collective_id=0, has_side_effects=True, vmem_limit_bytes=56 << 20
        ),
    )(
        block_table,
        context_len,
        partner,
        moved_slot,
        step_queries,
        step_keyvals,
        cache_pages,
        prompt_queries,
        prompt_keyvals,
        prompt_target,
    )


def local_plain(
    step_queries,
    step_keyvals,
    cache_pages,
    block_table,
    context_len,
    partner,
    moved_slot,
    prompt_queries,
    prompt_keyvals,
    prompt_target,
):
    inst_count = lax.axis_size("inst")
    tp_count = lax.axis_size("tp")
    me_inst = lax.axis_index("inst")
    me_tp = lax.axis_index("tp")
    requests = block_table.shape[0]
    kv_heads = step_keyvals.shape[2]
    head_dim = step_keyvals.shape[3] // 2
    rows_dev = prompt_queries.shape[0]
    capacity = max(2, 2 * rows_dev // inst_count)
    devices = inst_count * tp_count
    targets = prompt_target[:, 0].reshape(devices, rows_dev)
    mine = lax.dynamic_index_in_dim(targets, me_inst * tp_count + me_tp, 0, keepdims=False)
    onehot = (mine[:, None] == jnp.arange(inst_count, dtype=jnp.int32)[None, :]).astype(jnp.int32)
    rank = jnp.sum((jnp.cumsum(onehot, axis=0) - onehot) * onehot, axis=1)
    place = mine * capacity + rank
    dispatch = (
        jnp.arange(inst_count * capacity, dtype=jnp.int32)[:, None] == place[None, :]
    ).astype(jnp.bfloat16)
    send_queries = (
        jnp.dot(dispatch, prompt_queries, preferred_element_type=jnp.float32)
        .astype(jnp.bfloat16)
        .reshape(inst_count, capacity, -1)
    )
    flat_keyvals = prompt_keyvals.reshape(rows_dev, -1)
    send_keyvals = (
        jnp.dot(dispatch, flat_keyvals, preferred_element_type=jnp.float32)
        .astype(jnp.bfloat16)
        .reshape(inst_count, capacity, -1)
    )
    recv_queries, recv_keyvals = (
        lax.all_to_all(
            lax.all_to_all(send_queries, "inst", split_axis=0, concat_axis=0, tiled=True),
            "tp",
            split_axis=2,
            concat_axis=1,
            tiled=True,
        ),
        lax.all_to_all(
            lax.all_to_all(send_keyvals, "inst", split_axis=0, concat_axis=0, tiled=True),
            "tp",
            split_axis=2,
            concat_axis=1,
            tiled=True,
        ),
    )
    gathered = cache_pages[block_table]
    context = gathered.reshape(requests, -1, kv_heads, 2 * head_dim)
    lengths = lax.dynamic_slice_in_dim(context_len, me_inst * requests, requests)
    my_slot = moved_slot[me_inst]
    other = partner[me_inst]
    other_len = context_len[other * requests + moved_slot[other]]
    bit_total = inst_count.bit_length() - 1
    distance = jnp.bitwise_xor(me_inst, other)
    outgoing = lax.dynamic_index_in_dim(context, my_slot, 0, keepdims=False)
    incoming = outgoing
    for bit in range(bit_total):
        arrived = swapped(outgoing, "inst", bit)
        incoming = jnp.where(distance == 1 << bit, arrived, incoming)
    context = lax.dynamic_update_index_in_dim(context, incoming, my_slot, 0)
    lengths = lengths.at[my_slot].set(other_len)
    decode_output = decode_block(step_queries, context, lengths, step_keyvals)
    slots = inst_count * tp_count * capacity
    slot_queries = recv_queries.reshape(slots, -1)
    slot_keyvals = recv_keyvals.reshape(slots, kv_heads, 2 * head_dim)
    counts = jnp.sum((targets == me_inst).astype(jnp.int32), axis=1)
    valid = (jnp.arange(capacity, dtype=jnp.int32)[None, :] < counts[:, None]).reshape(slots)
    prefill_output = prefill_block(slot_queries, slot_keyvals, valid)
    return (decode_output, prefill_output)


def local(*arrays):
    rows_dev = arrays[7].shape[0]
    if (2 * rows_dev // lax.axis_size("inst")) % 8:
        return local_plain(*arrays)
    return local_fused(*arrays)


def solution(mesh):
    placed = (
        P(None, "inst", "tp"),
        P(None, "inst", "tp", None),
        P("inst", None, "tp", None),
        P("inst", None),
        P(),
        P(),
        P(),
        P(("inst", "tp"), None),
        P(("inst", "tp"), None, None),
        P(),
    )
    return jax.shard_map(
        local,
        mesh=mesh,
        in_specs=placed,
        out_specs=(P(None, "inst", "tp"), P("inst", "tp")),
        check_vma=False,
    )
```

```python
import functools
import math

import jax
import jax.numpy as jnp
from jax import lax
from jax.experimental import pallas as pl
from jax.experimental.pallas import tpu as pltpu
from jax.sharding import PartitionSpec as P


def swapped(array, axis, bit):
    return lax.ppermute(array, axis, [(i, i ^ 1 << bit) for i in range(lax.axis_size(axis))])


def masked_weights(scores, mask):
    shifted = jnp.where(mask, scores, jnp.float32(-1e30))
    top = jnp.max(shifted, axis=-1, keepdims=True)
    expo = jnp.where(mask, jnp.exp(shifted - top), jnp.float32(0.0))
    total = jnp.sum(expo, axis=-1, keepdims=True)
    total = jnp.where(total > 0, total, jnp.float32(1.0))
    return expo / total


def decode_block(queries, context, lengths, fresh):
    steps, count, width = queries.shape
    kv_heads = context.shape[2]
    head_dim = context.shape[3] // 2
    group = width // (kv_heads * head_dim)
    span = context.shape[1]
    scale = head_dim ** (-0.5)
    query = queries.reshape(steps, count, kv_heads, group, head_dim)
    past = (
        jnp.einsum(
            "trkgd,rckd->trkgc", query, context[..., :head_dim], preferred_element_type=jnp.float32
        )
        * scale
    )
    newer = (
        jnp.einsum(
            "trkgd,urkd->trkgu", query, fresh[..., :head_dim], preferred_element_type=jnp.float32
        )
        * scale
    )
    past_mask = (jnp.arange(span, dtype=jnp.int32)[None, :] < lengths[:, None])[
        None, :, None, None, :
    ]
    step_ids = jnp.arange(steps, dtype=jnp.int32)
    new_mask = (step_ids[None, :] <= step_ids[:, None])[:, None, None, None, :]
    mask = jnp.concatenate(
        [jnp.broadcast_to(past_mask, past.shape), jnp.broadcast_to(new_mask, newer.shape)], axis=-1
    )
    weights = masked_weights(jnp.concatenate([past, newer], axis=-1), mask).astype(jnp.bfloat16)
    out = jnp.einsum(
        "trkgc,rckd->trkgd",
        weights[..., :span],
        context[..., head_dim:],
        preferred_element_type=jnp.float32,
    )
    out = out + jnp.einsum(
        "trkgu,urkd->trkgd",
        weights[..., span:],
        fresh[..., head_dim:],
        preferred_element_type=jnp.float32,
    )
    return out.reshape(steps, count, width).astype(jnp.bfloat16)


def prefill_block(queries, keyvals, valid):
    slots, width = queries.shape
    kv_heads = keyvals.shape[1]
    head_dim = keyvals.shape[2] // 2
    group = width // (kv_heads * head_dim)
    scale = head_dim ** (-0.5)
    query = queries.reshape(slots, kv_heads, group, head_dim)
    block = 512 if slots % 512 == 0 else slots
    pieces = []
    for start in range(0, slots, block):
        finish = start + block
        scores = (
            jnp.einsum(
                "qkgd,ckd->kgqc",
                query[start:finish],
                keyvals[:finish, :, :head_dim],
                preferred_element_type=jnp.float32,
            )
            * scale
        )
        query_pos = jnp.arange(start, finish, dtype=jnp.int32)
        key_pos = jnp.arange(finish, dtype=jnp.int32)
        mask = (valid[None, :finish] & (key_pos[None, :] <= query_pos[:, None]))[None, None]
        weights = masked_weights(scores, jnp.broadcast_to(mask, scores.shape)).astype(jnp.bfloat16)
        out = jnp.einsum(
            "kgqc,ckd->qkgd",
            weights,
            keyvals[:finish, :, head_dim:],
            preferred_element_type=jnp.float32,
        )
        out = jnp.where(valid[start:finish, None, None, None], out, jnp.float32(0.0))
        pieces.append(out.reshape(block, width).astype(jnp.bfloat16))
    return jnp.concatenate(pieces, axis=0)


MESH = pl.DeviceIdType.MESH
NEG = -1e30


def fused_kernel(
    n_inst,
    n_tp,
    block_ref,
    length_ref,
    partner_ref,
    moved_ref,
    step_q_ref,
    step_kv_ref,
    cache_hbm,
    prompt_q_hbm,
    prompt_kv_ref,
    target_ref,
    decode_ref,
    prefill_ref,
    cache_ref,
    prompt_q_ref,
    send_ref,
    recv_ref,
    step_ref,
    context_ref,
    decoded_ref,
    move_q_out,
    move_kv_out,
    move_q_in,
    move_kv_in,
    move_o_out,
    move_o_in,
    bias_ref,
    filled_ref,
    part_ref,
    part_top_ref,
    cache_sem,
    prompt_sem,
    self_sem,
    send_sem,
    recv_sem,
    move_send_sem,
    move_recv_sem,
):
    f32, bf16 = jnp.float32, jnp.bfloat16
    me_inst, me_tp = lax.axis_index("inst"), lax.axis_index("tp")
    me = me_inst * n_tp + me_tp
    devices = n_inst * n_tp
    bits = n_inst.bit_length() - 1
    steps, requests, width = step_q_ref.shape
    kv_heads, both = step_kv_ref.shape[2:]
    head = both // 2
    heads = width // head
    group = heads // kv_heads
    rows = prompt_q_ref.shape[1]
    cap = recv_ref.shape[1]
    slots = devices * cap
    pages, page = block_ref.shape[1], cache_ref.shape[1]
    unit = group * head + both
    factor = head**-0.5 * math.log2(math.e)

    prompt_copies = [
        pltpu.make_async_copy(
            prompt_q_hbm.at[:, tp * width : (tp + 1) * width],
            prompt_q_ref.at[tp],
            prompt_sem.at[tp],
        )
        for tp in range(n_tp)
    ]
    for copy in prompt_copies:
        copy.start()
    cache_copy = pltpu.make_async_copy(cache_hbm, cache_ref, cache_sem)
    cache_copy.start()

    barrier = pltpu.get_barrier_semaphore()
    for turn in range(1, devices):
        inst = lax.rem(me_inst + turn // n_tp, n_inst)
        tp = lax.rem(me_tp + turn % n_tp, n_tp)
        pl.semaphore_signal(barrier, inc=1, device_id=(inst, tp), device_id_type=MESH)

    for t in range(steps):
        for h in range(heads):
            step_ref[t * heads + h] = step_q_ref[t, :, h * head : (h + 1) * head].astype(f32)
    my_slot = moved_ref[me_inst]
    distance = partner_ref[me_inst] - me_inst
    move_q_out[...] = step_ref[:, my_slot, :].astype(bf16)
    move_kv_out[...] = step_kv_ref[:, my_slot].reshape(steps * kv_heads, both)

    lanes = n_tp * rows
    mine = target_ref[pl.ds(me_inst, 1), :]
    onehot = (lax.broadcasted_iota(jnp.int32, (n_inst, lanes), 0) == mine).astype(f32)
    row_from = lax.broadcasted_iota(jnp.int32, (lanes, lanes), 0)
    row_to = lax.broadcasted_iota(jnp.int32, (lanes, lanes), 1)
    earlier = ((row_from < row_to) & (row_from // rows == row_to // rows)).astype(bf16)
    before = jnp.dot(onehot.astype(bf16), earlier, preferred_element_type=f32)
    rank = jnp.sum(before * onehot, axis=0, keepdims=True)
    place = mine.astype(f32) * cap + rank
    both_rows = (
        lax.broadcasted_iota(jnp.int32, (n_inst * cap, lanes), 0).astype(f32) == place
    ).astype(f32)
    dispatch = both_rows[:, :rows]
    for tp in range(1, n_tp):
        dispatch = jnp.where(me_tp == tp, both_rows[:, tp * rows : (tp + 1) * rows], dispatch)
    dispatch = dispatch.astype(bf16)

    def pack(tp):
        for h in range(kv_heads):
            start = h * group * head
            queries = prompt_q_ref[tp, :, start : start + group * head]
            packed = jnp.dot(dispatch, queries, preferred_element_type=f32)
            send_ref[tp, :, :, h * unit : h * unit + group * head] = packed.reshape(
                n_inst, cap, group * head
            ).astype(bf16)
            keyvals = prompt_kv_ref[:, tp * kv_heads + h, :]
            packed = jnp.dot(dispatch, keyvals, preferred_element_type=f32)
            send_ref[tp, :, :, h * unit + group * head : (h + 1) * unit] = packed.reshape(
                n_inst, cap, both
            ).astype(bf16)

    def neighbour(bit):
        return me_inst + (1 - 2 * lax.rem(me_inst // (1 << bit), 2)) * (1 << bit)

    def move(bit, source, target, which):
        return pltpu.make_async_remote_copy(
            src_ref=source,
            dst_ref=target.at[bit],
            send_sem=move_send_sem.at[which, bit],
            recv_sem=move_recv_sem.at[which, bit],
            device_id=(neighbour(bit), me_tp),
            device_id_type=MESH,
        )

    moves = []
    for bit in range(bits):
        moves.append(move(bit, move_q_out, move_q_in, 0))
        moves.append(move(bit, move_kv_out, move_kv_in, 1))

    def shipment(inst, tp, source):
        return pltpu.make_async_remote_copy(
            src_ref=send_ref.at[tp, inst],
            dst_ref=recv_ref.at[source],
            send_sem=send_sem.at[inst * n_tp + tp],
            recv_sem=recv_sem.at[source],
            device_id=(inst, tp),
            device_id_type=MESH,
        )

    half = n_inst // 2
    order = []
    for j in range(half):
        order.extend([half + j, j])
    for tp in range(n_tp):
        prompt_copies[tp].wait()
        pack(tp)
        if tp == 0:
            pl.semaphore_wait(barrier, devices - 1)
            for copy in moves:
                copy.start()
        for j in order:
            inst = lax.rem(me_inst + j, n_inst)
            if j:
                shipment(inst, tp, me).start()
            else:
                pl.when(me_tp != tp)(lambda: shipment(me_inst, tp, me).start())
    own = pltpu.make_async_copy(send_ref.at[me_tp, me_inst], recv_ref.at[me], self_sem)
    own.start()

    here = (target_ref[...] == me_inst).astype(bf16)
    slot = lax.broadcasted_iota(jnp.int32, (slots, 1), 0)
    spread = (
        slot // (n_tp * cap) == lax.broadcasted_iota(jnp.int32, (slots, n_inst), 1)
    ).astype(bf16)
    named = jnp.dot(spread, here, preferred_element_type=f32)
    lane = lax.broadcasted_iota(jnp.int32, (slots, lanes), 1)
    named = jnp.where(lane // rows == lax.rem(slot // cap, n_tp), named, 0.0)
    counts = jnp.sum(named, axis=1, keepdims=True)
    filled = (lax.rem(slot, cap).astype(f32) < counts).astype(f32)
    filled = jnp.broadcast_to(filled, (slots, head))
    filled_ref[...] = filled
    across = jnp.transpose(filled)[0:1, :]
    query_pos = lax.broadcasted_iota(jnp.int32, (slots, slots), 0)
    key_pos = lax.broadcasted_iota(jnp.int32, (slots, slots), 1)
    bias_ref[...] = jnp.where((key_pos <= query_pos) & (across > 0), 0.0, NEG)

    cache_copy.wait()
    for copy in moves:
        copy.wait()
    moved_q, moved_kv = move_q_in[0].astype(f32), move_kv_in[0].astype(f32)
    for bit in range(1, bits):
        match = (distance == (1 << bit)) | (distance == -(1 << bit))
        moved_q = jnp.where(match, move_q_in[bit].astype(f32), moved_q)
        moved_kv = jnp.where(match, move_kv_in[bit].astype(f32), moved_kv)
    moved_q, moved_kv = moved_q.astype(bf16), moved_kv.astype(bf16)

    queries_all = steps * heads
    span = pages * page * kv_heads
    fresh_all = steps * kv_heads
    query_row = lax.broadcasted_iota(jnp.int32, (queries_all, 1), 0)
    query_head = lax.rem(query_row, heads) // group
    query_step = query_row // heads
    past_col = lax.broadcasted_iota(jnp.int32, (1, span), 1)
    past_head, past_token = lax.rem(past_col, kv_heads), past_col // kv_heads
    fresh_col = lax.broadcasted_iota(jnp.int32, (1, fresh_all), 1)
    fresh_mask = (lax.rem(fresh_col, kv_heads) == query_head) & (
        fresh_col // kv_heads <= query_step
    )
    contract = (((1,), (1,)), ((), ()))

    def decode_slot(slot, carry):
        for i in range(pages):
            context_ref[i * page * kv_heads : (i + 1) * page * kv_heads, :] = cache_ref[
                block_ref[slot, i]
            ].reshape(page * kv_heads, both)
        is_moved = slot == my_slot
        queries = jnp.where(is_moved, moved_q, step_ref[:, slot, :].astype(bf16))
        fresh = jnp.where(
            is_moved, moved_kv, step_kv_ref[:, slot].reshape(fresh_all, both)
        )
        length = length_ref[me_inst * requests + slot]
        past = lax.dot_general(
            queries, context_ref[:, :head], contract, preferred_element_type=f32
        )
        newer = lax.dot_general(queries, fresh[:, :head], contract, preferred_element_type=f32)
        past = jnp.where((past_head == query_head) & (past_token < length), past, NEG)
        newer = jnp.where(fresh_mask, newer, NEG)
        top = jnp.maximum(
            jnp.max(past, axis=1, keepdims=True), jnp.max(newer, axis=1, keepdims=True)
        )
        past = jnp.exp2((past - top) * factor)
        newer = jnp.exp2((newer - top) * factor)
        total = jnp.sum(past, axis=1, keepdims=True) + jnp.sum(newer, axis=1, keepdims=True)
        share = 1.0 / total
        out = jnp.dot(
            (past * share).astype(bf16), context_ref[:, head:], preferred_element_type=f32
        )
        out = out + jnp.dot(
            (newer * share).astype(bf16), fresh[:, head:], preferred_element_type=f32
        )
        decoded_ref[:, slot, :] = out
        return carry

    lax.fori_loop(0, requests, decode_slot, 0)

    move_o_out[...] = decoded_ref[:, my_slot, :].astype(bf16)
    returns = [move(bit, move_o_out, move_o_in, 2) for bit in range(bits)]
    for copy in returns:
        copy.start()
    for copy in returns:
        copy.wait()
    moved_o = move_o_in[0].astype(f32)
    for bit in range(1, bits):
        match = (distance == (1 << bit)) | (distance == -(1 << bit))
        moved_o = jnp.where(match, move_o_in[bit].astype(f32), moved_o)
    slot_row = lax.broadcasted_iota(jnp.int32, (requests, 1), 0)
    for t in range(steps):
        for h in range(heads):
            row = t * heads + h
            decode_ref[t, :, h * head : (h + 1) * head] = jnp.where(
                slot_row == my_slot, moved_o[row : row + 1, :], decoded_ref[row]
            ).astype(bf16)

    size = slots // 2
    local_inst = lax.rem(me_inst, half)
    near_base = me_inst - local_inst
    far_base = half - near_base
    is_low = me_inst < half

    def take(part, column, count):
        first = part * (devices // 2)
        rows_in = recv_ref[
            first : first + devices // 2, :, pl.ds(pl.multiple_of(column, 128), count)
        ]
        return rows_in.astype(f32).reshape(size, count).astype(bf16)

    def keys_of(part, h):
        keyvals = take(part, h * unit + group * head, both)
        ones = jnp.ones((size, head), bf16)
        return keyvals[:, :head], jnp.concatenate([keyvals[:, head:], ones], axis=1)

    def attend(part, h, g, keys, values, first):
        queries = take(part, h * unit + g * head, head)
        scores = lax.dot_general(queries, keys, contract, preferred_element_type=f32)
        scores = scores + bias_ref[part * size : (part + 1) * size, pl.ds(first, keys.shape[0])]
        top = jnp.max(scores, axis=1, keepdims=True)
        return scores, top

    def finish(part, h, g, out):
        out = out[:, :head] / out[:, head:]
        out = jnp.where(filled_ref[part * size : (part + 1) * size, :] > 0, out, 0.0)
        column = pl.multiple_of((h * group + g) * head, 128)
        prefill_ref[part * size : (part + 1) * size, pl.ds(column, head)] = out.astype(bf16)

    def whole(part, h, g, keys, values):
        scores, top = attend(part, h, g, keys, values, 0)
        expo = jnp.exp2((scores - top) * factor).astype(bf16)
        finish(part, h, g, jnp.dot(expo, values, preferred_element_type=f32))

    def lower(h, carry):
        keys, values = keys_of(0, h)
        for g in range(group):
            whole(0, h, g, keys, values)
        return carry

    def upper_alone(h, carry):
        keys, values = keys_of(1, h)
        for g in range(group):
            scores, top = attend(1, h, g, keys, values, size)
            expo = jnp.exp2((scores - top) * factor).astype(bf16)
            part_ref[h * group + g] = jnp.dot(expo, values, preferred_element_type=f32)
            part_top_ref[h * group + g] = jnp.broadcast_to(top, (size, head))
        return carry

    def upper_all(h, carry):
        keys_0, values_0 = keys_of(0, h)
        keys_1, values_1 = keys_of(1, h)
        keys = jnp.concatenate([keys_0, keys_1], axis=0)
        values = jnp.concatenate([values_0, values_1], axis=0)
        for g in range(group):
            whole(1, h, g, keys, values)
        return carry

    def lower_then_upper(h, carry):
        keys, values = keys_of(0, h)
        for g in range(group):
            whole(0, h, g, keys, values)
            scores, top = attend(1, h, g, keys, values, 0)
            before_top = part_top_ref[h * group + g][:, :1]
            new_top = jnp.maximum(top, before_top)
            expo = jnp.exp2((scores - new_top) * factor).astype(bf16)
            out = jnp.dot(expo, values, preferred_element_type=f32)
            out = out + part_ref[h * group + g] * jnp.exp2((before_top - new_top) * factor)
            finish(1, h, g, out)
        return carry

    def loop(body):
        def run():
            lax.fori_loop(0, kv_heads, body, 0)

        return run

    own.wait()
    for j in range(half):
        for t in range(n_tp):
            if j or t:
                inst = near_base + lax.rem(local_inst + j, half)
                source = inst * n_tp + lax.rem(me_tp + t, n_tp)
                shipment(me_inst, me_tp, source).wait_recv()
    pl.when(is_low)(loop(lower))
    pl.when(jnp.logical_not(is_low))(loop(upper_alone))
    for j in range(half):
        for t in range(n_tp):
            inst = far_base + lax.rem(local_inst + j, half)
            source = inst * n_tp + lax.rem(me_tp + t, n_tp)
            shipment(me_inst, me_tp, source).wait_recv()
    pl.when(is_low)(loop(upper_all))
    pl.when(jnp.logical_not(is_low))(loop(lower_then_upper))

    for j in range(n_inst):
        for t in range(n_tp):
            if j or t:
                inst, tp = lax.rem(me_inst + j, n_inst), lax.rem(me_tp + t, n_tp)
                shipment(inst, tp, me).wait_send()


def local_fused(
    step_queries,
    step_keyvals,
    cache_pages,
    block_table,
    context_len,
    partner,
    moved_slot,
    prompt_queries,
    prompt_keyvals,
    prompt_target,
):
    n_inst, n_tp = lax.axis_size("inst"), lax.axis_size("tp")
    devices = n_inst * n_tp
    bits = n_inst.bit_length() - 1
    steps, requests, width = step_queries.shape
    kv_heads, both = step_keyvals.shape[2:]
    head = both // 2
    heads = width // head
    cap = 2 * prompt_queries.shape[0] // n_inst
    slots = devices * cap
    columns = width + kv_heads * both
    span = block_table.shape[1] * cache_pages.shape[1] * kv_heads
    bf16, f32 = jnp.bfloat16, jnp.float32
    smem = pl.BlockSpec(memory_space=pltpu.SMEM)
    vmem = pl.BlockSpec(memory_space=pltpu.VMEM)
    hbm = pl.BlockSpec(memory_space=pltpu.HBM)
    return pl.pallas_call(
        functools.partial(fused_kernel, n_inst, n_tp),
        out_shape=(
            pltpu.VMEM(step_queries.shape, bf16),
            pltpu.VMEM((slots, width), bf16),
        ),
        in_specs=[smem] * 4
        + [vmem, vmem, hbm, hbm, vmem, vmem],
        out_specs=(vmem, vmem),
        scratch_shapes=[
            pltpu.VMEM(cache_pages.shape, bf16),
            pltpu.VMEM((n_tp, prompt_queries.shape[0], width), bf16),
            pltpu.VMEM((n_tp, n_inst, cap, columns), bf16),
            pltpu.VMEM((devices, cap, columns), bf16),
            pltpu.VMEM((steps * heads, requests, head), f32),
            pltpu.VMEM((span, both), bf16),
            pltpu.VMEM((steps * heads, requests, head), f32),
            pltpu.VMEM((steps * heads, head), bf16),
            pltpu.VMEM((steps * kv_heads, both), bf16),
            pltpu.VMEM((bits, steps * heads, head), bf16),
            pltpu.VMEM((bits, steps * kv_heads, both), bf16),
            pltpu.VMEM((steps * heads, head), bf16),
            pltpu.VMEM((bits, steps * heads, head), bf16),
            pltpu.VMEM((slots, slots), f32),
            pltpu.VMEM((slots, head), f32),
            pltpu.VMEM((heads, slots // 2, both), f32),
            pltpu.VMEM((heads, slots // 2, head), f32),
            pltpu.SemaphoreType.DMA,
            pltpu.SemaphoreType.DMA((n_tp,)),
            pltpu.SemaphoreType.DMA,
            pltpu.SemaphoreType.DMA((devices,)),
            pltpu.SemaphoreType.DMA((devices,)),
            pltpu.SemaphoreType.DMA((3, bits)),
            pltpu.SemaphoreType.DMA((3, bits)),
        ],
        compiler_params=pltpu.CompilerParams(
            collective_id=0, has_side_effects=True, vmem_limit_bytes=58 << 20
        ),
    )(
        block_table,
        context_len,
        partner,
        moved_slot,
        step_queries,
        step_keyvals,
        cache_pages,
        prompt_queries,
        prompt_keyvals,
        prompt_target.reshape(n_inst, -1),
    )


def local_plain(
    step_queries,
    step_keyvals,
    cache_pages,
    block_table,
    context_len,
    partner,
    moved_slot,
    prompt_queries,
    prompt_keyvals,
    prompt_target,
):
    inst_count = lax.axis_size("inst")
    tp_count = lax.axis_size("tp")
    me_inst = lax.axis_index("inst")
    me_tp = lax.axis_index("tp")
    requests = block_table.shape[0]
    kv_heads = step_keyvals.shape[2]
    head_dim = step_keyvals.shape[3] // 2
    rows_dev = prompt_queries.shape[0]
    capacity = max(2, 2 * rows_dev // inst_count)
    devices = inst_count * tp_count
    targets = prompt_target[:, 0].reshape(devices, rows_dev)
    mine = lax.dynamic_index_in_dim(targets, me_inst * tp_count + me_tp, 0, keepdims=False)
    onehot = (mine[:, None] == jnp.arange(inst_count, dtype=jnp.int32)[None, :]).astype(jnp.int32)
    rank = jnp.sum((jnp.cumsum(onehot, axis=0) - onehot) * onehot, axis=1)
    place = mine * capacity + rank
    dispatch = (
        jnp.arange(inst_count * capacity, dtype=jnp.int32)[:, None] == place[None, :]
    ).astype(jnp.bfloat16)
    send_queries = (
        jnp.dot(dispatch, prompt_queries, preferred_element_type=jnp.float32)
        .astype(jnp.bfloat16)
        .reshape(inst_count, capacity, -1)
    )
    flat_keyvals = prompt_keyvals.reshape(rows_dev, -1)
    send_keyvals = (
        jnp.dot(dispatch, flat_keyvals, preferred_element_type=jnp.float32)
        .astype(jnp.bfloat16)
        .reshape(inst_count, capacity, -1)
    )
    recv_queries, recv_keyvals = (
        lax.all_to_all(
            lax.all_to_all(send_queries, "inst", split_axis=0, concat_axis=0, tiled=True),
            "tp",
            split_axis=2,
            concat_axis=1,
            tiled=True,
        ),
        lax.all_to_all(
            lax.all_to_all(send_keyvals, "inst", split_axis=0, concat_axis=0, tiled=True),
            "tp",
            split_axis=2,
            concat_axis=1,
            tiled=True,
        ),
    )
    gathered = cache_pages[block_table]
    context = gathered.reshape(requests, -1, kv_heads, 2 * head_dim)
    lengths = lax.dynamic_slice_in_dim(context_len, me_inst * requests, requests)
    my_slot = moved_slot[me_inst]
    other = partner[me_inst]
    other_len = context_len[other * requests + moved_slot[other]]
    bit_total = inst_count.bit_length() - 1
    distance = jnp.bitwise_xor(me_inst, other)
    outgoing = lax.dynamic_index_in_dim(context, my_slot, 0, keepdims=False)
    incoming = outgoing
    for bit in range(bit_total):
        arrived = swapped(outgoing, "inst", bit)
        incoming = jnp.where(distance == 1 << bit, arrived, incoming)
    context = lax.dynamic_update_index_in_dim(context, incoming, my_slot, 0)
    lengths = lengths.at[my_slot].set(other_len)
    decode_output = decode_block(step_queries, context, lengths, step_keyvals)
    slots = inst_count * tp_count * capacity
    slot_queries = recv_queries.reshape(slots, -1)
    slot_keyvals = recv_keyvals.reshape(slots, kv_heads, 2 * head_dim)
    counts = jnp.sum((targets == me_inst).astype(jnp.int32), axis=1)
    valid = (jnp.arange(capacity, dtype=jnp.int32)[None, :] < counts[:, None]).reshape(slots)
    prefill_output = prefill_block(slot_queries, slot_keyvals, valid)
    return (decode_output, prefill_output)


def local(*arrays):
    rows_dev = arrays[7].shape[0]
    if (2 * rows_dev // lax.axis_size("inst")) % 8:
        return local_plain(*arrays)
    return local_fused(*arrays)


def solution(mesh):
    placed = (
        P(None, "inst", "tp"),
        P(None, "inst", "tp", None),
        P("inst", None, "tp", None),
        P("inst", None),
        P(),
        P(),
        P(),
        P(("inst", "tp"), None),
        P(("inst", "tp"), None, None),
        P(),
    )
    return jax.shard_map(
        local,
        mesh=mesh,
        in_specs=placed,
        out_specs=(P(None, "inst", "tp"), P("inst", "tp")),
        check_vma=False,
    )
```

```python
import functools
import math

import jax
import jax.numpy as jnp
from jax import lax
from jax.experimental import pallas as pl
from jax.experimental.pallas import tpu as pltpu
from jax.sharding import PartitionSpec as P


def swapped(array, axis, bit):
    return lax.ppermute(array, axis, [(i, i ^ 1 << bit) for i in range(lax.axis_size(axis))])


def masked_weights(scores, mask):
    shifted = jnp.where(mask, scores, jnp.float32(-1e30))
    top = jnp.max(shifted, axis=-1, keepdims=True)
    expo = jnp.where(mask, jnp.exp(shifted - top), jnp.float32(0.0))
    total = jnp.sum(expo, axis=-1, keepdims=True)
    total = jnp.where(total > 0, total, jnp.float32(1.0))
    return expo / total


def decode_block(queries, context, lengths, fresh):
    steps, count, width = queries.shape
    kv_heads = context.shape[2]
    head_dim = context.shape[3] // 2
    group = width // (kv_heads * head_dim)
    span = context.shape[1]
    scale = head_dim ** (-0.5)
    query = queries.reshape(steps, count, kv_heads, group, head_dim)
    past = (
        jnp.einsum(
            "trkgd,rckd->trkgc", query, context[..., :head_dim], preferred_element_type=jnp.float32
        )
        * scale
    )
    newer = (
        jnp.einsum(
            "trkgd,urkd->trkgu", query, fresh[..., :head_dim], preferred_element_type=jnp.float32
        )
        * scale
    )
    past_mask = (jnp.arange(span, dtype=jnp.int32)[None, :] < lengths[:, None])[
        None, :, None, None, :
    ]
    step_ids = jnp.arange(steps, dtype=jnp.int32)
    new_mask = (step_ids[None, :] <= step_ids[:, None])[:, None, None, None, :]
    mask = jnp.concatenate(
        [jnp.broadcast_to(past_mask, past.shape), jnp.broadcast_to(new_mask, newer.shape)], axis=-1
    )
    weights = masked_weights(jnp.concatenate([past, newer], axis=-1), mask).astype(jnp.bfloat16)
    out = jnp.einsum(
        "trkgc,rckd->trkgd",
        weights[..., :span],
        context[..., head_dim:],
        preferred_element_type=jnp.float32,
    )
    out = out + jnp.einsum(
        "trkgu,urkd->trkgd",
        weights[..., span:],
        fresh[..., head_dim:],
        preferred_element_type=jnp.float32,
    )
    return out.reshape(steps, count, width).astype(jnp.bfloat16)


def prefill_block(queries, keyvals, valid):
    slots, width = queries.shape
    kv_heads = keyvals.shape[1]
    head_dim = keyvals.shape[2] // 2
    group = width // (kv_heads * head_dim)
    scale = head_dim ** (-0.5)
    query = queries.reshape(slots, kv_heads, group, head_dim)
    block = 512 if slots % 512 == 0 else slots
    pieces = []
    for start in range(0, slots, block):
        finish = start + block
        scores = (
            jnp.einsum(
                "qkgd,ckd->kgqc",
                query[start:finish],
                keyvals[:finish, :, :head_dim],
                preferred_element_type=jnp.float32,
            )
            * scale
        )
        query_pos = jnp.arange(start, finish, dtype=jnp.int32)
        key_pos = jnp.arange(finish, dtype=jnp.int32)
        mask = (valid[None, :finish] & (key_pos[None, :] <= query_pos[:, None]))[None, None]
        weights = masked_weights(scores, jnp.broadcast_to(mask, scores.shape)).astype(jnp.bfloat16)
        out = jnp.einsum(
            "kgqc,ckd->qkgd",
            weights,
            keyvals[:finish, :, head_dim:],
            preferred_element_type=jnp.float32,
        )
        out = jnp.where(valid[start:finish, None, None, None], out, jnp.float32(0.0))
        pieces.append(out.reshape(block, width).astype(jnp.bfloat16))
    return jnp.concatenate(pieces, axis=0)


MESH = pl.DeviceIdType.MESH
NEG = -1e30


def fused_kernel(
    n_inst,
    n_tp,
    block_ref,
    length_ref,
    partner_ref,
    moved_ref,
    step_q_ref,
    step_kv_ref,
    cache_hbm,
    prompt_q_hbm,
    prompt_kv_ref,
    target_ref,
    decode_ref,
    prefill_ref,
    cache_ref,
    prompt_q_ref,
    send_ref,
    recv_ref,
    step_ref,
    context_ref,
    decoded_ref,
    move_q_out,
    move_kv_out,
    move_q_in,
    move_kv_in,
    move_o_out,
    move_o_in,
    bias_ref,
    filled_ref,
    part_ref,
    part_top_ref,
    cache_sem,
    prompt_sem,
    self_sem,
    send_sem,
    recv_sem,
    move_send_sem,
    move_recv_sem,
):
    f32, bf16 = jnp.float32, jnp.bfloat16
    me_inst, me_tp = lax.axis_index("inst"), lax.axis_index("tp")
    me = me_inst * n_tp + me_tp
    devices = n_inst * n_tp
    bits = n_inst.bit_length() - 1
    steps, requests, width = step_q_ref.shape
    kv_heads, both = step_kv_ref.shape[2:]
    head = both // 2
    heads = width // head
    group = heads // kv_heads
    rows = prompt_q_ref.shape[1]
    cap = recv_ref.shape[1]
    slots = devices * cap
    pages, page = block_ref.shape[1], cache_ref.shape[1]
    unit = group * head + both
    factor = head**-0.5 * math.log2(math.e)

    prompt_copies = [
        pltpu.make_async_copy(
            prompt_q_hbm.at[:, tp * width : (tp + 1) * width],
            prompt_q_ref.at[tp],
            prompt_sem.at[tp],
        )
        for tp in range(n_tp)
    ]
    for copy in prompt_copies:
        copy.start()
    cache_copy = pltpu.make_async_copy(cache_hbm, cache_ref, cache_sem)
    cache_copy.start()

    barrier = pltpu.get_barrier_semaphore()
    for turn in range(1, devices):
        inst = lax.rem(me_inst + turn // n_tp, n_inst)
        tp = lax.rem(me_tp + turn % n_tp, n_tp)
        pl.semaphore_signal(barrier, inc=1, device_id=(inst, tp), device_id_type=MESH)

    for t in range(steps):
        for h in range(heads):
            step_ref[t * heads + h] = step_q_ref[t, :, h * head : (h + 1) * head].astype(f32)
    my_slot = moved_ref[me_inst]
    distance = partner_ref[me_inst] - me_inst
    move_q_out[...] = step_ref[:, my_slot, :].astype(bf16)
    move_kv_out[...] = step_kv_ref[:, my_slot].reshape(steps * kv_heads, both)

    lanes = n_tp * rows
    mine = target_ref[pl.ds(me_inst, 1), :]
    onehot = (lax.broadcasted_iota(jnp.int32, (n_inst, lanes), 0) == mine).astype(f32)
    row_from = lax.broadcasted_iota(jnp.int32, (lanes, lanes), 0)
    row_to = lax.broadcasted_iota(jnp.int32, (lanes, lanes), 1)
    earlier = ((row_from < row_to) & (row_from // rows == row_to // rows)).astype(bf16)
    before = jnp.dot(onehot.astype(bf16), earlier, preferred_element_type=f32)
    rank = jnp.sum(before * onehot, axis=0, keepdims=True)
    place = mine.astype(f32) * cap + rank
    both_rows = (
        lax.broadcasted_iota(jnp.int32, (n_inst * cap, lanes), 0).astype(f32) == place
    ).astype(f32)
    dispatch = both_rows[:, :rows]
    for tp in range(1, n_tp):
        dispatch = jnp.where(me_tp == tp, both_rows[:, tp * rows : (tp + 1) * rows], dispatch)
    dispatch = dispatch.astype(bf16)

    def pack(tp):
        for h in range(kv_heads):
            start = h * group * head
            queries = prompt_q_ref[tp, :, start : start + group * head]
            packed = jnp.dot(dispatch, queries, preferred_element_type=f32)
            send_ref[tp, :, :, h * unit : h * unit + group * head] = packed.reshape(
                n_inst, cap, group * head
            ).astype(bf16)
            keyvals = prompt_kv_ref[:, tp * kv_heads + h, :]
            packed = jnp.dot(dispatch, keyvals, preferred_element_type=f32)
            send_ref[tp, :, :, h * unit + group * head : (h + 1) * unit] = packed.reshape(
                n_inst, cap, both
            ).astype(bf16)

    def neighbour(bit):
        return me_inst + (1 - 2 * lax.rem(me_inst // (1 << bit), 2)) * (1 << bit)

    def move(bit, source, target, which):
        return pltpu.make_async_remote_copy(
            src_ref=source,
            dst_ref=target.at[bit],
            send_sem=move_send_sem.at[which, bit],
            recv_sem=move_recv_sem.at[which, bit],
            device_id=(neighbour(bit), me_tp),
            device_id_type=MESH,
        )

    moves = []
    for bit in range(bits):
        moves.append(move(bit, move_q_out, move_q_in, 0))
        moves.append(move(bit, move_kv_out, move_kv_in, 1))

    def shipment(inst, tp, source):
        return pltpu.make_async_remote_copy(
            src_ref=send_ref.at[tp, inst],
            dst_ref=recv_ref.at[source],
            send_sem=send_sem.at[inst * n_tp + tp],
            recv_sem=recv_sem.at[source],
            device_id=(inst, tp),
            device_id_type=MESH,
        )

    half = n_inst // 2
    order = []
    for j in range(half):
        order.extend([half + j, j])
    for tp in range(n_tp):
        prompt_copies[tp].wait()
        pack(tp)
        if tp == 0:
            pl.semaphore_wait(barrier, devices - 1)
            for copy in moves:
                copy.start()
        for j in order:
            inst = lax.rem(me_inst + j, n_inst)
            if j:
                shipment(inst, tp, me).start()
            else:
                pl.when(me_tp != tp)(lambda: shipment(me_inst, tp, me).start())
    own = pltpu.make_async_copy(send_ref.at[me_tp, me_inst], recv_ref.at[me], self_sem)
    own.start()

    here = (target_ref[...] == me_inst).astype(bf16)
    slot = lax.broadcasted_iota(jnp.int32, (slots, 1), 0)
    spread = (
        slot // (n_tp * cap) == lax.broadcasted_iota(jnp.int32, (slots, n_inst), 1)
    ).astype(bf16)
    named = jnp.dot(spread, here, preferred_element_type=f32)
    lane = lax.broadcasted_iota(jnp.int32, (slots, lanes), 1)
    named = jnp.where(lane // rows == lax.rem(slot // cap, n_tp), named, 0.0)
    counts = jnp.sum(named, axis=1, keepdims=True)
    filled = (lax.rem(slot, cap).astype(f32) < counts).astype(f32)
    filled = jnp.broadcast_to(filled, (slots, head))
    filled_ref[...] = filled
    across = jnp.transpose(filled)[0:1, :]
    query_pos = lax.broadcasted_iota(jnp.int32, (slots, slots), 0)
    key_pos = lax.broadcasted_iota(jnp.int32, (slots, slots), 1)
    bias_ref[...] = jnp.where((key_pos <= query_pos) & (across > 0), 0.0, NEG)

    cache_copy.wait()
    for copy in moves:
        copy.wait()
    moved_q, moved_kv = move_q_in[0].astype(f32), move_kv_in[0].astype(f32)
    for bit in range(1, bits):
        match = (distance == (1 << bit)) | (distance == -(1 << bit))
        moved_q = jnp.where(match, move_q_in[bit].astype(f32), moved_q)
        moved_kv = jnp.where(match, move_kv_in[bit].astype(f32), moved_kv)
    moved_q, moved_kv = moved_q.astype(bf16), moved_kv.astype(bf16)

    queries_all = steps * heads
    span = pages * page * kv_heads
    fresh_all = steps * kv_heads
    query_row = lax.broadcasted_iota(jnp.int32, (queries_all, 1), 0)
    query_head = lax.rem(query_row, heads) // group
    query_step = query_row // heads
    past_col = lax.broadcasted_iota(jnp.int32, (1, span), 1)
    past_head = lax.rem(past_col, kv_heads)
    page_row = lax.rem(past_col, page * kv_heads)
    past_token = (
        past_col // (page * kv_heads) * page
        + page_row // (2 * kv_heads)
        + lax.rem(page_row // kv_heads, 2) * (page // 2)
    )
    fresh_col = lax.broadcasted_iota(jnp.int32, (1, fresh_all), 1)
    fresh_mask = (lax.rem(fresh_col, kv_heads) == query_head) & (
        fresh_col // kv_heads <= query_step
    )
    contract = (((1,), (1,)), ((), ()))

    def decode_slot(slot, carry):
        for i in range(pages):
            tokens = cache_ref[block_ref[slot, i]].astype(f32)
            paired = jnp.concatenate([tokens[: page // 2], tokens[page // 2 :]], axis=1)
            context_ref[i * page * kv_heads : (i + 1) * page * kv_heads, :] = paired.reshape(
                page * kv_heads, both
            ).astype(bf16)
        is_moved = slot == my_slot
        queries = jnp.where(is_moved, moved_q, step_ref[:, slot, :].astype(bf16))
        fresh = jnp.where(
            is_moved, moved_kv, step_kv_ref[:, slot].reshape(fresh_all, both)
        )
        length = length_ref[me_inst * requests + slot]
        past = lax.dot_general(
            queries, context_ref[:, :head], contract, preferred_element_type=f32
        )
        newer = lax.dot_general(queries, fresh[:, :head], contract, preferred_element_type=f32)
        past = jnp.where((past_head == query_head) & (past_token < length), past, NEG)
        newer = jnp.where(fresh_mask, newer, NEG)
        top = jnp.maximum(
            jnp.max(past, axis=1, keepdims=True), jnp.max(newer, axis=1, keepdims=True)
        )
        past = jnp.exp2((past - top) * factor)
        newer = jnp.exp2((newer - top) * factor)
        total = jnp.sum(past, axis=1, keepdims=True) + jnp.sum(newer, axis=1, keepdims=True)
        share = 1.0 / total
        out = jnp.dot(
            (past * share).astype(bf16), context_ref[:, head:], preferred_element_type=f32
        )
        out = out + jnp.dot(
            (newer * share).astype(bf16), fresh[:, head:], preferred_element_type=f32
        )
        decoded_ref[:, slot, :] = out
        return carry

    lax.fori_loop(0, requests, decode_slot, 0)

    move_o_out[...] = decoded_ref[:, my_slot, :].astype(bf16)
    returns = [move(bit, move_o_out, move_o_in, 2) for bit in range(bits)]
    for copy in returns:
        copy.start()
    for copy in returns:
        copy.wait()
    moved_o = move_o_in[0].astype(f32)
    for bit in range(1, bits):
        match = (distance == (1 << bit)) | (distance == -(1 << bit))
        moved_o = jnp.where(match, move_o_in[bit].astype(f32), moved_o)
    slot_row = lax.broadcasted_iota(jnp.int32, (requests, 1), 0)
    for t in range(steps):
        for h in range(heads):
            row = t * heads + h
            decode_ref[t, :, h * head : (h + 1) * head] = jnp.where(
                slot_row == my_slot, moved_o[row : row + 1, :], decoded_ref[row]
            ).astype(bf16)

    size = slots // 2
    local_inst = lax.rem(me_inst, half)
    near_base = me_inst - local_inst
    far_base = half - near_base
    is_low = me_inst < half

    def take(part, column, count):
        first = part * (devices // 2)
        rows_in = recv_ref[
            first : first + devices // 2, :, pl.ds(pl.multiple_of(column, 128), count)
        ]
        return rows_in.astype(f32).reshape(size, count).astype(bf16)

    def keys_of(part, h):
        keyvals = take(part, h * unit + group * head, both)
        ones = jnp.ones((size, head), bf16)
        return keyvals[:, :head], jnp.concatenate([keyvals[:, head:], ones], axis=1)

    def attend(part, h, keys, first):
        queries = take(part, h * unit, group * head)
        queries = jnp.concatenate(
            [queries[:, g * head : (g + 1) * head] for g in range(group)], axis=0
        )
        scores = lax.dot_general(queries, keys, contract, preferred_element_type=f32)
        count = keys.shape[0]
        bias = bias_ref[part * size : (part + 1) * size, first : first + count]
        scores = (scores.reshape(group, size, count) + bias[None]).reshape(group * size, count)
        return scores, jnp.max(scores, axis=1, keepdims=True)

    def weigh(scores, top, values):
        expo = jnp.exp2((scores - top) * factor).astype(bf16)
        return jnp.dot(expo, values, preferred_element_type=f32)

    def finish(part, h, out):
        out = out[:, :head] / out[:, head:]
        keep = filled_ref[part * size : (part + 1) * size, :] > 0
        for g in range(group):
            column = pl.multiple_of((h * group + g) * head, 128)
            prefill_ref[part * size : (part + 1) * size, pl.ds(column, head)] = jnp.where(
                keep, out[g * size : (g + 1) * size], 0.0
            ).astype(bf16)

    def lower(h, carry):
        keys, values = keys_of(0, h)
        scores, top = attend(0, h, keys, 0)
        finish(0, h, weigh(scores, top, values))
        return carry

    def upper_alone(h, carry):
        keys, values = keys_of(1, h)
        scores, top = attend(1, h, keys, size)
        part_ref[h] = weigh(scores, top, values)
        part_top_ref[h] = jnp.broadcast_to(top, (group * size, head))
        return carry

    def upper_all(h, carry):
        keys_0, values_0 = keys_of(0, h)
        keys_1, values_1 = keys_of(1, h)
        keys = jnp.concatenate([keys_0, keys_1], axis=0)
        values = jnp.concatenate([values_0, values_1], axis=0)
        scores, top = attend(1, h, keys, 0)
        finish(1, h, weigh(scores, top, values))
        return carry

    def lower_then_upper(h, carry):
        keys, values = keys_of(0, h)
        scores, top = attend(0, h, keys, 0)
        finish(0, h, weigh(scores, top, values))
        scores, top = attend(1, h, keys, 0)
        old_top = part_top_ref[h]
        new_top = jnp.maximum(old_top, top)
        out = weigh(scores, new_top[:, :1], values)
        decay = jnp.exp2((old_top - new_top) * factor)
        out = out + part_ref[h] * jnp.concatenate([decay, decay], axis=1)
        finish(1, h, out)
        return carry

    def loop(body):
        def run():
            lax.fori_loop(0, kv_heads, body, 0)

        return run

    own.wait()
    for j in range(half):
        for t in range(n_tp):
            if j or t:
                inst = near_base + lax.rem(local_inst + j, half)
                source = inst * n_tp + lax.rem(me_tp + t, n_tp)
                shipment(me_inst, me_tp, source).wait_recv()
    pl.when(is_low)(loop(lower))
    pl.when(jnp.logical_not(is_low))(loop(upper_alone))
    for j in range(half):
        for t in range(n_tp):
            inst = far_base + lax.rem(local_inst + j, half)
            source = inst * n_tp + lax.rem(me_tp + t, n_tp)
            shipment(me_inst, me_tp, source).wait_recv()
    pl.when(is_low)(loop(upper_all))
    pl.when(jnp.logical_not(is_low))(loop(lower_then_upper))

    for j in range(n_inst):
        for t in range(n_tp):
            if j or t:
                inst, tp = lax.rem(me_inst + j, n_inst), lax.rem(me_tp + t, n_tp)
                shipment(inst, tp, me).wait_send()


def local_fused(
    step_queries,
    step_keyvals,
    cache_pages,
    block_table,
    context_len,
    partner,
    moved_slot,
    prompt_queries,
    prompt_keyvals,
    prompt_target,
):
    n_inst, n_tp = lax.axis_size("inst"), lax.axis_size("tp")
    devices = n_inst * n_tp
    bits = n_inst.bit_length() - 1
    steps, requests, width = step_queries.shape
    kv_heads, both = step_keyvals.shape[2:]
    head = both // 2
    heads = width // head
    cap = 2 * prompt_queries.shape[0] // n_inst
    slots = devices * cap
    columns = width + kv_heads * both
    span = block_table.shape[1] * cache_pages.shape[1] * kv_heads
    bf16, f32 = jnp.bfloat16, jnp.float32
    smem = pl.BlockSpec(memory_space=pltpu.SMEM)
    vmem = pl.BlockSpec(memory_space=pltpu.VMEM)
    hbm = pl.BlockSpec(memory_space=pltpu.HBM)
    return pl.pallas_call(
        functools.partial(fused_kernel, n_inst, n_tp),
        out_shape=(
            pltpu.VMEM(step_queries.shape, bf16),
            pltpu.VMEM((slots, width), bf16),
        ),
        in_specs=[smem] * 4
        + [vmem, vmem, hbm, hbm, vmem, vmem],
        out_specs=(vmem, vmem),
        scratch_shapes=[
            pltpu.VMEM(cache_pages.shape, bf16),
            pltpu.VMEM((n_tp, prompt_queries.shape[0], width), bf16),
            pltpu.VMEM((n_tp, n_inst, cap, columns), bf16),
            pltpu.VMEM((devices, cap, columns), bf16),
            pltpu.VMEM((steps * heads, requests, head), f32),
            pltpu.VMEM((span, both), bf16),
            pltpu.VMEM((steps * heads, requests, head), f32),
            pltpu.VMEM((steps * heads, head), bf16),
            pltpu.VMEM((steps * kv_heads, both), bf16),
            pltpu.VMEM((bits, steps * heads, head), bf16),
            pltpu.VMEM((bits, steps * kv_heads, both), bf16),
            pltpu.VMEM((steps * heads, head), bf16),
            pltpu.VMEM((bits, steps * heads, head), bf16),
            pltpu.VMEM((slots, slots), f32),
            pltpu.VMEM((slots, head), f32),
            pltpu.VMEM((kv_heads, heads // kv_heads * slots // 2, both), f32),
            pltpu.VMEM((kv_heads, heads // kv_heads * slots // 2, head), f32),
            pltpu.SemaphoreType.DMA,
            pltpu.SemaphoreType.DMA((n_tp,)),
            pltpu.SemaphoreType.DMA,
            pltpu.SemaphoreType.DMA((devices,)),
            pltpu.SemaphoreType.DMA((devices,)),
            pltpu.SemaphoreType.DMA((3, bits)),
            pltpu.SemaphoreType.DMA((3, bits)),
        ],
        compiler_params=pltpu.CompilerParams(
            collective_id=0, has_side_effects=True, vmem_limit_bytes=58 << 20
        ),
    )(
        block_table,
        context_len,
        partner,
        moved_slot,
        step_queries,
        step_keyvals,
        cache_pages,
        prompt_queries,
        prompt_keyvals,
        prompt_target.reshape(n_inst, -1),
    )


def local_plain(
    step_queries,
    step_keyvals,
    cache_pages,
    block_table,
    context_len,
    partner,
    moved_slot,
    prompt_queries,
    prompt_keyvals,
    prompt_target,
):
    inst_count = lax.axis_size("inst")
    tp_count = lax.axis_size("tp")
    me_inst = lax.axis_index("inst")
    me_tp = lax.axis_index("tp")
    requests = block_table.shape[0]
    kv_heads = step_keyvals.shape[2]
    head_dim = step_keyvals.shape[3] // 2
    rows_dev = prompt_queries.shape[0]
    capacity = max(2, 2 * rows_dev // inst_count)
    devices = inst_count * tp_count
    targets = prompt_target[:, 0].reshape(devices, rows_dev)
    mine = lax.dynamic_index_in_dim(targets, me_inst * tp_count + me_tp, 0, keepdims=False)
    onehot = (mine[:, None] == jnp.arange(inst_count, dtype=jnp.int32)[None, :]).astype(jnp.int32)
    rank = jnp.sum((jnp.cumsum(onehot, axis=0) - onehot) * onehot, axis=1)
    place = mine * capacity + rank
    dispatch = (
        jnp.arange(inst_count * capacity, dtype=jnp.int32)[:, None] == place[None, :]
    ).astype(jnp.bfloat16)
    send_queries = (
        jnp.dot(dispatch, prompt_queries, preferred_element_type=jnp.float32)
        .astype(jnp.bfloat16)
        .reshape(inst_count, capacity, -1)
    )
    flat_keyvals = prompt_keyvals.reshape(rows_dev, -1)
    send_keyvals = (
        jnp.dot(dispatch, flat_keyvals, preferred_element_type=jnp.float32)
        .astype(jnp.bfloat16)
        .reshape(inst_count, capacity, -1)
    )
    recv_queries, recv_keyvals = (
        lax.all_to_all(
            lax.all_to_all(send_queries, "inst", split_axis=0, concat_axis=0, tiled=True),
            "tp",
            split_axis=2,
            concat_axis=1,
            tiled=True,
        ),
        lax.all_to_all(
            lax.all_to_all(send_keyvals, "inst", split_axis=0, concat_axis=0, tiled=True),
            "tp",
            split_axis=2,
            concat_axis=1,
            tiled=True,
        ),
    )
    gathered = cache_pages[block_table]
    context = gathered.reshape(requests, -1, kv_heads, 2 * head_dim)
    lengths = lax.dynamic_slice_in_dim(context_len, me_inst * requests, requests)
    my_slot = moved_slot[me_inst]
    other = partner[me_inst]
    other_len = context_len[other * requests + moved_slot[other]]
    bit_total = inst_count.bit_length() - 1
    distance = jnp.bitwise_xor(me_inst, other)
    outgoing = lax.dynamic_index_in_dim(context, my_slot, 0, keepdims=False)
    incoming = outgoing
    for bit in range(bit_total):
        arrived = swapped(outgoing, "inst", bit)
        incoming = jnp.where(distance == 1 << bit, arrived, incoming)
    context = lax.dynamic_update_index_in_dim(context, incoming, my_slot, 0)
    lengths = lengths.at[my_slot].set(other_len)
    decode_output = decode_block(step_queries, context, lengths, step_keyvals)
    slots = inst_count * tp_count * capacity
    slot_queries = recv_queries.reshape(slots, -1)
    slot_keyvals = recv_keyvals.reshape(slots, kv_heads, 2 * head_dim)
    counts = jnp.sum((targets == me_inst).astype(jnp.int32), axis=1)
    valid = (jnp.arange(capacity, dtype=jnp.int32)[None, :] < counts[:, None]).reshape(slots)
    prefill_output = prefill_block(slot_queries, slot_keyvals, valid)
    return (decode_output, prefill_output)


def local(*arrays):
    rows_dev = arrays[7].shape[0]
    if (2 * rows_dev // lax.axis_size("inst")) % 8:
        return local_plain(*arrays)
    return local_fused(*arrays)


def solution(mesh):
    placed = (
        P(None, "inst", "tp"),
        P(None, "inst", "tp", None),
        P("inst", None, "tp", None),
        P("inst", None),
        P(),
        P(),
        P(),
        P(("inst", "tp"), None),
        P(("inst", "tp"), None, None),
        P(),
    )
    return jax.shard_map(
        local,
        mesh=mesh,
        in_specs=placed,
        out_specs=(P(None, "inst", "tp"), P("inst", "tp")),
        check_vma=False,
    )
```

```python
import functools
import math

import jax
import jax.numpy as jnp
from jax import lax
from jax.experimental import pallas as pl
from jax.experimental.pallas import tpu as pltpu
from jax.sharding import PartitionSpec as P


def swapped(array, axis, bit):
    return lax.ppermute(array, axis, [(i, i ^ 1 << bit) for i in range(lax.axis_size(axis))])


def masked_weights(scores, mask):
    shifted = jnp.where(mask, scores, jnp.float32(-1e30))
    top = jnp.max(shifted, axis=-1, keepdims=True)
    expo = jnp.where(mask, jnp.exp(shifted - top), jnp.float32(0.0))
    total = jnp.sum(expo, axis=-1, keepdims=True)
    total = jnp.where(total > 0, total, jnp.float32(1.0))
    return expo / total


def decode_block(queries, context, lengths, fresh):
    steps, count, width = queries.shape
    kv_heads = context.shape[2]
    head_dim = context.shape[3] // 2
    group = width // (kv_heads * head_dim)
    span = context.shape[1]
    scale = head_dim ** (-0.5)
    query = queries.reshape(steps, count, kv_heads, group, head_dim)
    past = (
        jnp.einsum(
            "trkgd,rckd->trkgc", query, context[..., :head_dim], preferred_element_type=jnp.float32
        )
        * scale
    )
    newer = (
        jnp.einsum(
            "trkgd,urkd->trkgu", query, fresh[..., :head_dim], preferred_element_type=jnp.float32
        )
        * scale
    )
    past_mask = (jnp.arange(span, dtype=jnp.int32)[None, :] < lengths[:, None])[
        None, :, None, None, :
    ]
    step_ids = jnp.arange(steps, dtype=jnp.int32)
    new_mask = (step_ids[None, :] <= step_ids[:, None])[:, None, None, None, :]
    mask = jnp.concatenate(
        [jnp.broadcast_to(past_mask, past.shape), jnp.broadcast_to(new_mask, newer.shape)], axis=-1
    )
    weights = masked_weights(jnp.concatenate([past, newer], axis=-1), mask).astype(jnp.bfloat16)
    out = jnp.einsum(
        "trkgc,rckd->trkgd",
        weights[..., :span],
        context[..., head_dim:],
        preferred_element_type=jnp.float32,
    )
    out = out + jnp.einsum(
        "trkgu,urkd->trkgd",
        weights[..., span:],
        fresh[..., head_dim:],
        preferred_element_type=jnp.float32,
    )
    return out.reshape(steps, count, width).astype(jnp.bfloat16)


def prefill_block(queries, keyvals, valid):
    slots, width = queries.shape
    kv_heads = keyvals.shape[1]
    head_dim = keyvals.shape[2] // 2
    group = width // (kv_heads * head_dim)
    scale = head_dim ** (-0.5)
    query = queries.reshape(slots, kv_heads, group, head_dim)
    block = 512 if slots % 512 == 0 else slots
    pieces = []
    for start in range(0, slots, block):
        finish = start + block
        scores = (
            jnp.einsum(
                "qkgd,ckd->kgqc",
                query[start:finish],
                keyvals[:finish, :, :head_dim],
                preferred_element_type=jnp.float32,
            )
            * scale
        )
        query_pos = jnp.arange(start, finish, dtype=jnp.int32)
        key_pos = jnp.arange(finish, dtype=jnp.int32)
        mask = (valid[None, :finish] & (key_pos[None, :] <= query_pos[:, None]))[None, None]
        weights = masked_weights(scores, jnp.broadcast_to(mask, scores.shape)).astype(jnp.bfloat16)
        out = jnp.einsum(
            "kgqc,ckd->qkgd",
            weights,
            keyvals[:finish, :, head_dim:],
            preferred_element_type=jnp.float32,
        )
        out = jnp.where(valid[start:finish, None, None, None], out, jnp.float32(0.0))
        pieces.append(out.reshape(block, width).astype(jnp.bfloat16))
    return jnp.concatenate(pieces, axis=0)


MESH = pl.DeviceIdType.MESH
NEG = -1e30


def fused_kernel(
    n_inst,
    n_tp,
    block_ref,
    length_ref,
    partner_ref,
    moved_ref,
    step_q_ref,
    step_kv_ref,
    cache_hbm,
    prompt_q_hbm,
    prompt_kv_ref,
    target_ref,
    decode_ref,
    prefill_ref,
    cache_ref,
    prompt_q_ref,
    send_ref,
    recv_ref,
    step_ref,
    context_ref,
    decoded_ref,
    move_q_out,
    move_kv_out,
    move_q_in,
    move_kv_in,
    move_o_out,
    move_o_in,
    bias_ref,
    filled_ref,
    part_ref,
    part_top_ref,
    cache_sem,
    prompt_sem,
    self_sem,
    send_sem,
    recv_sem,
    move_send_sem,
    move_recv_sem,
):
    f32, bf16 = jnp.float32, jnp.bfloat16
    me_inst, me_tp = lax.axis_index("inst"), lax.axis_index("tp")
    me = me_inst * n_tp + me_tp
    devices = n_inst * n_tp
    bits = n_inst.bit_length() - 1
    steps, requests, width = step_q_ref.shape
    kv_heads, both = step_kv_ref.shape[2:]
    head = both // 2
    heads = width // head
    group = heads // kv_heads
    rows = prompt_q_ref.shape[1]
    cap = recv_ref.shape[1]
    slots = devices * cap
    pages, page = block_ref.shape[1], cache_ref.shape[1]
    unit = group * head + both
    factor = head**-0.5 * math.log2(math.e)

    prompt_copies = [
        pltpu.make_async_copy(
            prompt_q_hbm.at[:, tp * width : (tp + 1) * width],
            prompt_q_ref.at[tp],
            prompt_sem.at[tp],
        )
        for tp in range(n_tp)
    ]
    for copy in prompt_copies:
        copy.start()
    cache_copy = pltpu.make_async_copy(cache_hbm, cache_ref, cache_sem)
    cache_copy.start()

    barrier = pltpu.get_barrier_semaphore()
    for turn in range(1, devices):
        inst = lax.rem(me_inst + turn // n_tp, n_inst)
        tp = lax.rem(me_tp + turn % n_tp, n_tp)
        pl.semaphore_signal(barrier, inc=1, device_id=(inst, tp), device_id_type=MESH)

    lanes = n_tp * rows
    mine = target_ref[pl.ds(me_inst, 1), :]
    onehot = (lax.broadcasted_iota(jnp.int32, (n_inst, lanes), 0) == mine).astype(f32)
    row_from = lax.broadcasted_iota(jnp.int32, (lanes, lanes), 0)
    row_to = lax.broadcasted_iota(jnp.int32, (lanes, lanes), 1)
    earlier = ((row_from < row_to) & (row_from // rows == row_to // rows)).astype(bf16)
    before = jnp.dot(onehot.astype(bf16), earlier, preferred_element_type=f32)
    rank = jnp.sum(before * onehot, axis=0, keepdims=True)
    place = mine.astype(f32) * cap + rank
    both_rows = (
        lax.broadcasted_iota(jnp.int32, (n_inst * cap, lanes), 0).astype(f32) == place
    ).astype(f32)
    dispatch = both_rows[:, :rows]
    for tp in range(1, n_tp):
        dispatch = jnp.where(me_tp == tp, both_rows[:, tp * rows : (tp + 1) * rows], dispatch)

    half = n_inst // 2
    local_inst = lax.rem(me_inst, half)
    near_base = me_inst - local_inst
    far_base = half - near_base
    is_low = me_inst < half
    low, high = dispatch[: half * cap], dispatch[half * cap :]
    far_rows = jnp.where(is_low, high, low).astype(bf16)
    near_rows = jnp.where(is_low, low, high).astype(bf16)

    def pack(tp, base, chosen):
        insts = pl.ds(base, half)
        for h in range(kv_heads):
            start = h * group * head
            queries = prompt_q_ref[tp, :, start : start + group * head]
            packed = jnp.dot(chosen, queries, preferred_element_type=f32)
            send_ref[tp, insts, :, h * unit : h * unit + group * head] = packed.reshape(
                half, cap, group * head
            ).astype(bf16)
            keyvals = prompt_kv_ref[:, tp * kv_heads + h, :]
            packed = jnp.dot(chosen, keyvals, preferred_element_type=f32)
            send_ref[tp, insts, :, h * unit + group * head : (h + 1) * unit] = packed.reshape(
                half, cap, both
            ).astype(bf16)

    my_slot = moved_ref[me_inst]
    distance = partner_ref[me_inst] - me_inst

    def prepare_moves():
        for t in range(steps):
            for h in range(heads):
                step_ref[t * heads + h] = step_q_ref[t, :, h * head : (h + 1) * head].astype(f32)
        move_q_out[...] = step_ref[:, my_slot, :].astype(bf16)
        move_kv_out[...] = step_kv_ref[:, my_slot].reshape(steps * kv_heads, both)

    def neighbour(bit):
        return me_inst + (1 - 2 * lax.rem(me_inst // (1 << bit), 2)) * (1 << bit)

    def move(bit, source, target, which):
        return pltpu.make_async_remote_copy(
            src_ref=source,
            dst_ref=target.at[bit],
            send_sem=move_send_sem.at[which, bit],
            recv_sem=move_recv_sem.at[which, bit],
            device_id=(neighbour(bit), me_tp),
            device_id_type=MESH,
        )

    moves = []
    for bit in range(bits):
        moves.append(move(bit, move_q_out, move_q_in, 0))
        moves.append(move(bit, move_kv_out, move_kv_in, 1))

    def shipment(inst, tp, source):
        return pltpu.make_async_remote_copy(
            src_ref=send_ref.at[tp, inst],
            dst_ref=recv_ref.at[source],
            send_sem=send_sem.at[inst * n_tp + tp],
            recv_sem=recv_sem.at[source],
            device_id=(inst, tp),
            device_id_type=MESH,
        )

    for tp in range(n_tp):
        prompt_copies[tp].wait()
        pack(tp, far_base, far_rows)
        if tp == 0:
            pl.semaphore_wait(barrier, devices - 1)
        for j in range(half):
            shipment(far_base + lax.rem(local_inst + j, half), tp, me).start()
        if tp == 0:
            prepare_moves()
            for copy in moves:
                copy.start()
        pack(tp, near_base, near_rows)
        for j in range(1, half):
            shipment(near_base + lax.rem(local_inst + j, half), tp, me).start()
        pl.when(me_tp != tp)(lambda: shipment(me_inst, tp, me).start())
    own = pltpu.make_async_copy(send_ref.at[me_tp, me_inst], recv_ref.at[me], self_sem)
    own.start()

    here = (target_ref[...] == me_inst).astype(bf16)
    slot = lax.broadcasted_iota(jnp.int32, (slots, 1), 0)
    spread = (
        slot // (n_tp * cap) == lax.broadcasted_iota(jnp.int32, (slots, n_inst), 1)
    ).astype(bf16)
    named = jnp.dot(spread, here, preferred_element_type=f32)
    lane = lax.broadcasted_iota(jnp.int32, (slots, lanes), 1)
    named = jnp.where(lane // rows == lax.rem(slot // cap, n_tp), named, 0.0)
    counts = jnp.sum(named, axis=1, keepdims=True)
    filled = (lax.rem(slot, cap).astype(f32) < counts).astype(f32)
    filled = jnp.broadcast_to(filled, (slots, head))
    filled_ref[...] = filled
    across = jnp.transpose(filled)[0:1, :]
    query_pos = lax.broadcasted_iota(jnp.int32, (slots, slots), 0)
    key_pos = lax.broadcasted_iota(jnp.int32, (slots, slots), 1)
    bias_ref[...] = jnp.where((key_pos <= query_pos) & (across > 0), 0.0, NEG)

    cache_copy.wait()
    for copy in moves:
        copy.wait()
    moved_q, moved_kv = move_q_in[0].astype(f32), move_kv_in[0].astype(f32)
    for bit in range(1, bits):
        match = (distance == (1 << bit)) | (distance == -(1 << bit))
        moved_q = jnp.where(match, move_q_in[bit].astype(f32), moved_q)
        moved_kv = jnp.where(match, move_kv_in[bit].astype(f32), moved_kv)
    moved_q, moved_kv = moved_q.astype(bf16), moved_kv.astype(bf16)

    queries_all = steps * heads
    span = pages * page * kv_heads
    fresh_all = steps * kv_heads
    query_row = lax.broadcasted_iota(jnp.int32, (queries_all, 1), 0)
    query_head = lax.rem(query_row, heads) // group
    query_step = query_row // heads
    past_col = lax.broadcasted_iota(jnp.int32, (1, span), 1)
    past_head = lax.rem(past_col, kv_heads)
    page_row = lax.rem(past_col, page * kv_heads)
    past_token = (
        past_col // (page * kv_heads) * page
        + page_row // (2 * kv_heads)
        + lax.rem(page_row // kv_heads, 2) * (page // 2)
    )
    fresh_col = lax.broadcasted_iota(jnp.int32, (1, fresh_all), 1)
    fresh_mask = (lax.rem(fresh_col, kv_heads) == query_head) & (
        fresh_col // kv_heads <= query_step
    )
    contract = (((1,), (1,)), ((), ()))

    def decode_slot(slot, carry):
        for i in range(pages):
            tokens = cache_ref[block_ref[slot, i]].astype(f32)
            paired = jnp.concatenate([tokens[: page // 2], tokens[page // 2 :]], axis=1)
            context_ref[i * page * kv_heads : (i + 1) * page * kv_heads, :] = paired.reshape(
                page * kv_heads, both
            ).astype(bf16)
        is_moved = slot == my_slot
        queries = jnp.where(is_moved, moved_q, step_ref[:, slot, :].astype(bf16))
        fresh = jnp.where(
            is_moved, moved_kv, step_kv_ref[:, slot].reshape(fresh_all, both)
        )
        length = length_ref[me_inst * requests + slot]
        past = lax.dot_general(
            queries, context_ref[:, :head], contract, preferred_element_type=f32
        )
        newer = lax.dot_general(queries, fresh[:, :head], contract, preferred_element_type=f32)
        past = jnp.where((past_head == query_head) & (past_token < length), past, NEG)
        newer = jnp.where(fresh_mask, newer, NEG)
        top = jnp.maximum(
            jnp.max(past, axis=1, keepdims=True), jnp.max(newer, axis=1, keepdims=True)
        )
        past = jnp.exp2((past - top) * factor)
        newer = jnp.exp2((newer - top) * factor)
        total = jnp.sum(past, axis=1, keepdims=True) + jnp.sum(newer, axis=1, keepdims=True)
        share = 1.0 / total
        out = jnp.dot(
            (past * share).astype(bf16), context_ref[:, head:], preferred_element_type=f32
        )
        out = out + jnp.dot(
            (newer * share).astype(bf16), fresh[:, head:], preferred_element_type=f32
        )
        decoded_ref[:, slot, :] = out
        return carry

    lax.fori_loop(0, requests, decode_slot, 0)

    move_o_out[...] = decoded_ref[:, my_slot, :].astype(bf16)
    returns = [move(bit, move_o_out, move_o_in, 2) for bit in range(bits)]
    for copy in returns:
        copy.start()

    size = slots // 2

    def take(part, column, count):
        first = part * (devices // 2)
        rows_in = recv_ref[
            first : first + devices // 2, :, pl.ds(pl.multiple_of(column, 128), count)
        ]
        return rows_in.astype(f32).reshape(size, count).astype(bf16)

    def keys_of(part, h):
        keyvals = take(part, h * unit + group * head, both)
        ones = jnp.ones((size, head), bf16)
        return keyvals[:, :head], jnp.concatenate([keyvals[:, head:], ones], axis=1)

    def attend(part, h, keys, first):
        queries = take(part, h * unit, group * head)
        queries = jnp.concatenate(
            [queries[:, g * head : (g + 1) * head] for g in range(group)], axis=0
        )
        scores = lax.dot_general(queries, keys, contract, preferred_element_type=f32)
        count = keys.shape[0]
        bias = bias_ref[part * size : (part + 1) * size, first : first + count]
        scores = (scores.reshape(group, size, count) + bias[None]).reshape(group * size, count)
        return scores, jnp.max(scores, axis=1, keepdims=True)

    def weigh(scores, top, values):
        expo = jnp.exp2((scores - top) * factor).astype(bf16)
        return jnp.dot(expo, values, preferred_element_type=f32)

    def finish(part, h, out):
        out = out[:, :head] / out[:, head:]
        keep = filled_ref[part * size : (part + 1) * size, :] > 0
        for g in range(group):
            column = pl.multiple_of((h * group + g) * head, 128)
            prefill_ref[part * size : (part + 1) * size, pl.ds(column, head)] = jnp.where(
                keep, out[g * size : (g + 1) * size], 0.0
            ).astype(bf16)

    def lower(h, carry):
        keys, values = keys_of(0, h)
        scores, top = attend(0, h, keys, 0)
        finish(0, h, weigh(scores, top, values))
        return carry

    def upper_alone(h, carry):
        keys, values = keys_of(1, h)
        scores, top = attend(1, h, keys, size)
        part_ref[h] = weigh(scores, top, values)
        part_top_ref[h] = jnp.broadcast_to(top, (group * size, head))
        return carry

    def upper_all(h, carry):
        keys_0, values_0 = keys_of(0, h)
        keys_1, values_1 = keys_of(1, h)
        keys = jnp.concatenate([keys_0, keys_1], axis=0)
        values = jnp.concatenate([values_0, values_1], axis=0)
        scores, top = attend(1, h, keys, 0)
        finish(1, h, weigh(scores, top, values))
        return carry

    def lower_then_upper(h, carry):
        keys, values = keys_of(0, h)
        scores, top = attend(0, h, keys, 0)
        finish(0, h, weigh(scores, top, values))
        scores, top = attend(1, h, keys, 0)
        old_top = part_top_ref[h]
        new_top = jnp.maximum(old_top, top)
        out = weigh(scores, new_top[:, :1], values)
        decay = jnp.exp2((old_top - new_top) * factor)
        out = out + part_ref[h] * jnp.concatenate([decay, decay], axis=1)
        finish(1, h, out)
        return carry

    def loop(body):
        def run():
            lax.fori_loop(0, kv_heads, body, 0)

        return run

    own.wait()
    for j in range(half):
        for t in range(n_tp):
            if j or t:
                inst = near_base + lax.rem(local_inst + j, half)
                source = inst * n_tp + lax.rem(me_tp + t, n_tp)
                shipment(me_inst, me_tp, source).wait_recv()
    pl.when(is_low)(loop(lower))
    pl.when(jnp.logical_not(is_low))(loop(upper_alone))
    for j in range(half):
        for t in range(n_tp):
            inst = far_base + lax.rem(local_inst + j, half)
            source = inst * n_tp + lax.rem(me_tp + t, n_tp)
            shipment(me_inst, me_tp, source).wait_recv()
    pl.when(is_low)(loop(upper_all))
    pl.when(jnp.logical_not(is_low))(loop(lower_then_upper))

    for copy in returns:
        copy.wait()
    moved_o = move_o_in[0].astype(f32)
    for bit in range(1, bits):
        match = (distance == (1 << bit)) | (distance == -(1 << bit))
        moved_o = jnp.where(match, move_o_in[bit].astype(f32), moved_o)
    slot_row = lax.broadcasted_iota(jnp.int32, (requests, 1), 0)
    for t in range(steps):
        for h in range(heads):
            row = t * heads + h
            decode_ref[t, :, h * head : (h + 1) * head] = jnp.where(
                slot_row == my_slot, moved_o[row : row + 1, :], decoded_ref[row]
            ).astype(bf16)

    for j in range(n_inst):
        for t in range(n_tp):
            if j or t:
                inst, tp = lax.rem(me_inst + j, n_inst), lax.rem(me_tp + t, n_tp)
                shipment(inst, tp, me).wait_send()


def local_fused(
    step_queries,
    step_keyvals,
    cache_pages,
    block_table,
    context_len,
    partner,
    moved_slot,
    prompt_queries,
    prompt_keyvals,
    prompt_target,
):
    n_inst, n_tp = lax.axis_size("inst"), lax.axis_size("tp")
    devices = n_inst * n_tp
    bits = n_inst.bit_length() - 1
    steps, requests, width = step_queries.shape
    kv_heads, both = step_keyvals.shape[2:]
    head = both // 2
    heads = width // head
    cap = 2 * prompt_queries.shape[0] // n_inst
    slots = devices * cap
    columns = width + kv_heads * both
    span = block_table.shape[1] * cache_pages.shape[1] * kv_heads
    bf16, f32 = jnp.bfloat16, jnp.float32
    smem = pl.BlockSpec(memory_space=pltpu.SMEM)
    vmem = pl.BlockSpec(memory_space=pltpu.VMEM)
    hbm = pl.BlockSpec(memory_space=pltpu.HBM)
    return pl.pallas_call(
        functools.partial(fused_kernel, n_inst, n_tp),
        out_shape=(
            pltpu.VMEM(step_queries.shape, bf16),
            pltpu.VMEM((slots, width), bf16),
        ),
        in_specs=[smem] * 4
        + [vmem, vmem, hbm, hbm, vmem, vmem],
        out_specs=(vmem, vmem),
        scratch_shapes=[
            pltpu.VMEM(cache_pages.shape, bf16),
            pltpu.VMEM((n_tp, prompt_queries.shape[0], width), bf16),
            pltpu.VMEM((n_tp, n_inst, cap, columns), bf16),
            pltpu.VMEM((devices, cap, columns), bf16),
            pltpu.VMEM((steps * heads, requests, head), f32),
            pltpu.VMEM((span, both), bf16),
            pltpu.VMEM((steps * heads, requests, head), f32),
            pltpu.VMEM((steps * heads, head), bf16),
            pltpu.VMEM((steps * kv_heads, both), bf16),
            pltpu.VMEM((bits, steps * heads, head), bf16),
            pltpu.VMEM((bits, steps * kv_heads, both), bf16),
            pltpu.VMEM((steps * heads, head), bf16),
            pltpu.VMEM((bits, steps * heads, head), bf16),
            pltpu.VMEM((slots, slots), f32),
            pltpu.VMEM((slots, head), f32),
            pltpu.VMEM((kv_heads, heads // kv_heads * slots // 2, both), f32),
            pltpu.VMEM((kv_heads, heads // kv_heads * slots // 2, head), f32),
            pltpu.SemaphoreType.DMA,
            pltpu.SemaphoreType.DMA((n_tp,)),
            pltpu.SemaphoreType.DMA,
            pltpu.SemaphoreType.DMA((devices,)),
            pltpu.SemaphoreType.DMA((devices,)),
            pltpu.SemaphoreType.DMA((3, bits)),
            pltpu.SemaphoreType.DMA((3, bits)),
        ],
        compiler_params=pltpu.CompilerParams(
            collective_id=0, has_side_effects=True, vmem_limit_bytes=58 << 20
        ),
    )(
        block_table,
        context_len,
        partner,
        moved_slot,
        step_queries,
        step_keyvals,
        cache_pages,
        prompt_queries,
        prompt_keyvals,
        prompt_target.reshape(n_inst, -1),
    )


def local_plain(
    step_queries,
    step_keyvals,
    cache_pages,
    block_table,
    context_len,
    partner,
    moved_slot,
    prompt_queries,
    prompt_keyvals,
    prompt_target,
):
    inst_count = lax.axis_size("inst")
    tp_count = lax.axis_size("tp")
    me_inst = lax.axis_index("inst")
    me_tp = lax.axis_index("tp")
    requests = block_table.shape[0]
    kv_heads = step_keyvals.shape[2]
    head_dim = step_keyvals.shape[3] // 2
    rows_dev = prompt_queries.shape[0]
    capacity = max(2, 2 * rows_dev // inst_count)
    devices = inst_count * tp_count
    targets = prompt_target[:, 0].reshape(devices, rows_dev)
    mine = lax.dynamic_index_in_dim(targets, me_inst * tp_count + me_tp, 0, keepdims=False)
    onehot = (mine[:, None] == jnp.arange(inst_count, dtype=jnp.int32)[None, :]).astype(jnp.int32)
    rank = jnp.sum((jnp.cumsum(onehot, axis=0) - onehot) * onehot, axis=1)
    place = mine * capacity + rank
    dispatch = (
        jnp.arange(inst_count * capacity, dtype=jnp.int32)[:, None] == place[None, :]
    ).astype(jnp.bfloat16)
    send_queries = (
        jnp.dot(dispatch, prompt_queries, preferred_element_type=jnp.float32)
        .astype(jnp.bfloat16)
        .reshape(inst_count, capacity, -1)
    )
    flat_keyvals = prompt_keyvals.reshape(rows_dev, -1)
    send_keyvals = (
        jnp.dot(dispatch, flat_keyvals, preferred_element_type=jnp.float32)
        .astype(jnp.bfloat16)
        .reshape(inst_count, capacity, -1)
    )
    recv_queries, recv_keyvals = (
        lax.all_to_all(
            lax.all_to_all(send_queries, "inst", split_axis=0, concat_axis=0, tiled=True),
            "tp",
            split_axis=2,
            concat_axis=1,
            tiled=True,
        ),
        lax.all_to_all(
            lax.all_to_all(send_keyvals, "inst", split_axis=0, concat_axis=0, tiled=True),
            "tp",
            split_axis=2,
            concat_axis=1,
            tiled=True,
        ),
    )
    gathered = cache_pages[block_table]
    context = gathered.reshape(requests, -1, kv_heads, 2 * head_dim)
    lengths = lax.dynamic_slice_in_dim(context_len, me_inst * requests, requests)
    my_slot = moved_slot[me_inst]
    other = partner[me_inst]
    other_len = context_len[other * requests + moved_slot[other]]
    bit_total = inst_count.bit_length() - 1
    distance = jnp.bitwise_xor(me_inst, other)
    outgoing = lax.dynamic_index_in_dim(context, my_slot, 0, keepdims=False)
    incoming = outgoing
    for bit in range(bit_total):
        arrived = swapped(outgoing, "inst", bit)
        incoming = jnp.where(distance == 1 << bit, arrived, incoming)
    context = lax.dynamic_update_index_in_dim(context, incoming, my_slot, 0)
    lengths = lengths.at[my_slot].set(other_len)
    decode_output = decode_block(step_queries, context, lengths, step_keyvals)
    slots = inst_count * tp_count * capacity
    slot_queries = recv_queries.reshape(slots, -1)
    slot_keyvals = recv_keyvals.reshape(slots, kv_heads, 2 * head_dim)
    counts = jnp.sum((targets == me_inst).astype(jnp.int32), axis=1)
    valid = (jnp.arange(capacity, dtype=jnp.int32)[None, :] < counts[:, None]).reshape(slots)
    prefill_output = prefill_block(slot_queries, slot_keyvals, valid)
    return (decode_output, prefill_output)


def local(*arrays):
    rows_dev = arrays[7].shape[0]
    if (2 * rows_dev // lax.axis_size("inst")) % 8:
        return local_plain(*arrays)
    return local_fused(*arrays)


def solution(mesh):
    placed = (
        P(None, "inst", "tp"),
        P(None, "inst", "tp", None),
        P("inst", None, "tp", None),
        P("inst", None),
        P(),
        P(),
        P(),
        P(("inst", "tp"), None),
        P(("inst", "tp"), None, None),
        P(),
    )
    return jax.shard_map(
        local,
        mesh=mesh,
        in_specs=placed,
        out_specs=(P(None, "inst", "tp"), P("inst", "tp")),
        check_vma=False,
    )
```

```python
import functools
import math

import jax
import jax.numpy as jnp
from jax import lax
from jax.experimental import pallas as pl
from jax.experimental.pallas import tpu as pltpu
from jax.sharding import PartitionSpec as P


def swapped(array, axis, bit):
    return lax.ppermute(array, axis, [(i, i ^ 1 << bit) for i in range(lax.axis_size(axis))])


def masked_weights(scores, mask):
    shifted = jnp.where(mask, scores, jnp.float32(-1e30))
    top = jnp.max(shifted, axis=-1, keepdims=True)
    expo = jnp.where(mask, jnp.exp(shifted - top), jnp.float32(0.0))
    total = jnp.sum(expo, axis=-1, keepdims=True)
    total = jnp.where(total > 0, total, jnp.float32(1.0))
    return expo / total


def decode_block(queries, context, lengths, fresh):
    steps, count, width = queries.shape
    kv_heads = context.shape[2]
    head_dim = context.shape[3] // 2
    group = width // (kv_heads * head_dim)
    span = context.shape[1]
    scale = head_dim ** (-0.5)
    query = queries.reshape(steps, count, kv_heads, group, head_dim)
    past = (
        jnp.einsum(
            "trkgd,rckd->trkgc", query, context[..., :head_dim], preferred_element_type=jnp.float32
        )
        * scale
    )
    newer = (
        jnp.einsum(
            "trkgd,urkd->trkgu", query, fresh[..., :head_dim], preferred_element_type=jnp.float32
        )
        * scale
    )
    past_mask = (jnp.arange(span, dtype=jnp.int32)[None, :] < lengths[:, None])[
        None, :, None, None, :
    ]
    step_ids = jnp.arange(steps, dtype=jnp.int32)
    new_mask = (step_ids[None, :] <= step_ids[:, None])[:, None, None, None, :]
    mask = jnp.concatenate(
        [jnp.broadcast_to(past_mask, past.shape), jnp.broadcast_to(new_mask, newer.shape)], axis=-1
    )
    weights = masked_weights(jnp.concatenate([past, newer], axis=-1), mask).astype(jnp.bfloat16)
    out = jnp.einsum(
        "trkgc,rckd->trkgd",
        weights[..., :span],
        context[..., head_dim:],
        preferred_element_type=jnp.float32,
    )
    out = out + jnp.einsum(
        "trkgu,urkd->trkgd",
        weights[..., span:],
        fresh[..., head_dim:],
        preferred_element_type=jnp.float32,
    )
    return out.reshape(steps, count, width).astype(jnp.bfloat16)


def prefill_block(queries, keyvals, valid):
    slots, width = queries.shape
    kv_heads = keyvals.shape[1]
    head_dim = keyvals.shape[2] // 2
    group = width // (kv_heads * head_dim)
    scale = head_dim ** (-0.5)
    query = queries.reshape(slots, kv_heads, group, head_dim)
    block = 512 if slots % 512 == 0 else slots
    pieces = []
    for start in range(0, slots, block):
        finish = start + block
        scores = (
            jnp.einsum(
                "qkgd,ckd->kgqc",
                query[start:finish],
                keyvals[:finish, :, :head_dim],
                preferred_element_type=jnp.float32,
            )
            * scale
        )
        query_pos = jnp.arange(start, finish, dtype=jnp.int32)
        key_pos = jnp.arange(finish, dtype=jnp.int32)
        mask = (valid[None, :finish] & (key_pos[None, :] <= query_pos[:, None]))[None, None]
        weights = masked_weights(scores, jnp.broadcast_to(mask, scores.shape)).astype(jnp.bfloat16)
        out = jnp.einsum(
            "kgqc,ckd->qkgd",
            weights,
            keyvals[:finish, :, head_dim:],
            preferred_element_type=jnp.float32,
        )
        out = jnp.where(valid[start:finish, None, None, None], out, jnp.float32(0.0))
        pieces.append(out.reshape(block, width).astype(jnp.bfloat16))
    return jnp.concatenate(pieces, axis=0)


MESH = pl.DeviceIdType.MESH
NEG = -1e30


def fused_kernel(
    n_inst,
    n_tp,
    block_ref,
    length_ref,
    partner_ref,
    moved_ref,
    step_q_hbm,
    step_kv_hbm,
    cache_hbm,
    prompt_q_hbm,
    prompt_kv_hbm,
    target_ref,
    decode_ref,
    prefill_ref,
    cache_ref,
    step_q_ref,
    step_kv_ref,
    prompt_q_ref,
    prompt_kv_ref,
    send_ref,
    recv_ref,
    step_ref,
    context_ref,
    decoded_ref,
    move_q_out,
    move_kv_out,
    move_q_in,
    move_kv_in,
    move_o_out,
    move_o_in,
    bias_ref,
    filled_ref,
    part_ref,
    part_top_ref,
    cache_sem,
    small_sem,
    prompt_sem,
    self_sem,
    send_sem,
    recv_sem,
    move_send_sem,
    move_recv_sem,
):
    f32, bf16 = jnp.float32, jnp.bfloat16
    me_inst, me_tp = lax.axis_index("inst"), lax.axis_index("tp")
    me = me_inst * n_tp + me_tp
    devices = n_inst * n_tp
    bits = n_inst.bit_length() - 1
    steps, requests, width = step_q_hbm.shape
    kv_heads, both = step_kv_ref.shape[2:]
    head = both // 2
    heads = width // head
    group = heads // kv_heads
    rows = prompt_q_ref.shape[1]
    cap = recv_ref.shape[1]
    slots = devices * cap
    pages, page = block_ref.shape[1], cache_ref.shape[1]
    unit = group * head + both
    factor = head**-0.5 * math.log2(math.e)

    tps = [lax.rem(me_tp + t, n_tp) for t in range(n_tp)]
    prompt_copies = [
        pltpu.make_async_copy(
            prompt_q_hbm.at[:, pl.ds(pl.multiple_of(tps[t] * width, 128), width)],
            prompt_q_ref.at[t],
            prompt_sem.at[t],
        )
        for t in range(n_tp)
    ]
    small_copies = [
        pltpu.make_async_copy(source, target, small_sem.at[i])
        for i, (source, target) in enumerate(
            [
                (prompt_kv_hbm, prompt_kv_ref),
                (step_q_hbm, step_q_ref),
                (step_kv_hbm, step_kv_ref),
            ]
        )
    ]
    small_copies[0].start()
    for copy in prompt_copies:
        copy.start()
    for copy in small_copies[1:]:
        copy.start()
    cache_copy = pltpu.make_async_copy(cache_hbm, cache_ref, cache_sem)
    cache_copy.start()

    barrier = pltpu.get_barrier_semaphore()
    for turn in range(1, devices):
        inst = lax.rem(me_inst + turn // n_tp, n_inst)
        tp = lax.rem(me_tp + turn % n_tp, n_tp)
        pl.semaphore_signal(barrier, inc=1, device_id=(inst, tp), device_id_type=MESH)

    lanes = n_tp * rows
    mine = target_ref[pl.ds(me_inst, 1), :]
    onehot = (lax.broadcasted_iota(jnp.int32, (n_inst, lanes), 0) == mine).astype(f32)
    row_from = lax.broadcasted_iota(jnp.int32, (lanes, lanes), 0)
    row_to = lax.broadcasted_iota(jnp.int32, (lanes, lanes), 1)
    earlier = ((row_from < row_to) & (row_from // rows == row_to // rows)).astype(bf16)
    before = jnp.dot(onehot.astype(bf16), earlier, preferred_element_type=f32)
    rank = jnp.sum(before * onehot, axis=0, keepdims=True)
    place = mine.astype(f32) * cap + rank
    both_rows = (
        lax.broadcasted_iota(jnp.int32, (n_inst * cap, lanes), 0).astype(f32) == place
    ).astype(f32)
    dispatch = both_rows[:, :rows]
    for tp in range(1, n_tp):
        dispatch = jnp.where(me_tp == tp, both_rows[:, tp * rows : (tp + 1) * rows], dispatch)

    half = n_inst // 2
    local_inst = lax.rem(me_inst, half)
    near_base = me_inst - local_inst
    far_base = half - near_base
    is_low = me_inst < half
    low, high = dispatch[: half * cap], dispatch[half * cap :]
    far_rows = jnp.where(is_low, high, low).astype(bf16)
    near_rows = jnp.where(is_low, low, high).astype(bf16)

    def pack(t, base, chosen):
        insts = pl.ds(base, half)
        for h in range(kv_heads):
            start = h * group * head
            queries = prompt_q_ref[t, :, start : start + group * head]
            packed = jnp.dot(chosen, queries, preferred_element_type=f32)
            send_ref[tps[t], insts, :, h * unit : h * unit + group * head] = packed.reshape(
                half, cap, group * head
            ).astype(bf16)
            keyvals = prompt_kv_ref[:, h, :]
            for tp in range(1, n_tp):
                keyvals = jnp.where(
                    tps[t] == tp, prompt_kv_ref[:, tp * kv_heads + h, :], keyvals
                )
            packed = jnp.dot(chosen, keyvals, preferred_element_type=f32)
            send_ref[tps[t], insts, :, h * unit + group * head : (h + 1) * unit] = (
                packed.reshape(half, cap, both).astype(bf16)
            )

    my_slot = moved_ref[me_inst]
    distance = partner_ref[me_inst] - me_inst

    def prepare_moves():
        for copy in small_copies[1:]:
            copy.wait()
        for t in range(steps):
            for h in range(heads):
                step_ref[t * heads + h] = step_q_ref[t, :, h * head : (h + 1) * head].astype(f32)
        move_q_out[...] = step_ref[:, my_slot, :].astype(bf16)
        move_kv_out[...] = step_kv_ref[:, my_slot].reshape(steps * kv_heads, both)

    def neighbour(bit):
        return me_inst + (1 - 2 * lax.rem(me_inst // (1 << bit), 2)) * (1 << bit)

    def move(bit, source, target, which):
        return pltpu.make_async_remote_copy(
            src_ref=source,
            dst_ref=target.at[bit],
            send_sem=move_send_sem.at[which, bit],
            recv_sem=move_recv_sem.at[which, bit],
            device_id=(neighbour(bit), me_tp),
            device_id_type=MESH,
        )

    moves = []
    for bit in range(bits):
        moves.append(move(bit, move_q_out, move_q_in, 0))
        moves.append(move(bit, move_kv_out, move_kv_in, 1))

    def shipment(inst, tp, source):
        return pltpu.make_async_remote_copy(
            src_ref=send_ref.at[tp, inst],
            dst_ref=recv_ref.at[source],
            send_sem=send_sem.at[inst * n_tp + tp],
            recv_sem=recv_sem.at[source],
            device_id=(inst, tp),
            device_id_type=MESH,
        )

    small_copies[0].wait()
    for t in range(n_tp):
        prompt_copies[t].wait()
        pack(t, far_base, far_rows)
        if t == 0:
            pl.semaphore_wait(barrier, devices - 1)
        for j in range(half):
            shipment(far_base + lax.rem(local_inst + j, half), tps[t], me).start()
        if t == 0:
            prepare_moves()
            for copy in moves:
                copy.start()
        pack(t, near_base, near_rows)
        for j in range(half):
            if j or t:
                shipment(near_base + lax.rem(local_inst + j, half), tps[t], me).start()
    own = pltpu.make_async_copy(send_ref.at[me_tp, me_inst], recv_ref.at[me], self_sem)
    own.start()

    here = (target_ref[...] == me_inst).astype(bf16)
    slot = lax.broadcasted_iota(jnp.int32, (slots, 1), 0)
    spread = (
        slot // (n_tp * cap) == lax.broadcasted_iota(jnp.int32, (slots, n_inst), 1)
    ).astype(bf16)
    named = jnp.dot(spread, here, preferred_element_type=f32)
    lane = lax.broadcasted_iota(jnp.int32, (slots, lanes), 1)
    named = jnp.where(lane // rows == lax.rem(slot // cap, n_tp), named, 0.0)
    counts = jnp.sum(named, axis=1, keepdims=True)
    filled = (lax.rem(slot, cap).astype(f32) < counts).astype(f32)
    filled = jnp.broadcast_to(filled, (slots, head))
    filled_ref[...] = filled
    across = jnp.transpose(filled)[0:1, :]
    query_pos = lax.broadcasted_iota(jnp.int32, (slots, slots), 0)
    key_pos = lax.broadcasted_iota(jnp.int32, (slots, slots), 1)
    bias_ref[...] = jnp.where((key_pos <= query_pos) & (across > 0), 0.0, NEG)

    cache_copy.wait()
    for copy in moves:
        copy.wait()
    moved_q, moved_kv = move_q_in[0].astype(f32), move_kv_in[0].astype(f32)
    for bit in range(1, bits):
        match = (distance == (1 << bit)) | (distance == -(1 << bit))
        moved_q = jnp.where(match, move_q_in[bit].astype(f32), moved_q)
        moved_kv = jnp.where(match, move_kv_in[bit].astype(f32), moved_kv)
    moved_q, moved_kv = moved_q.astype(bf16), moved_kv.astype(bf16)

    queries_all = steps * heads
    span = pages * page * kv_heads
    fresh_all = steps * kv_heads
    query_row = lax.broadcasted_iota(jnp.int32, (queries_all, 1), 0)
    query_head = lax.rem(query_row, heads) // group
    query_step = query_row // heads
    past_col = lax.broadcasted_iota(jnp.int32, (1, span), 1)
    past_head = lax.rem(past_col, kv_heads)
    page_row = lax.rem(past_col, page * kv_heads)
    past_token = (
        past_col // (page * kv_heads) * page
        + page_row // (2 * kv_heads)
        + lax.rem(page_row // kv_heads, 2) * (page // 2)
    )
    fresh_col = lax.broadcasted_iota(jnp.int32, (1, fresh_all), 1)
    fresh_mask = (lax.rem(fresh_col, kv_heads) == query_head) & (
        fresh_col // kv_heads <= query_step
    )
    contract = (((1,), (1,)), ((), ()))

    def decode_slot(slot, carry):
        for i in range(pages):
            tokens = cache_ref[block_ref[slot, i]].astype(f32)
            paired = jnp.concatenate([tokens[: page // 2], tokens[page // 2 :]], axis=1)
            context_ref[i * page * kv_heads : (i + 1) * page * kv_heads, :] = paired.reshape(
                page * kv_heads, both
            ).astype(bf16)
        is_moved = slot == my_slot
        queries = jnp.where(is_moved, moved_q, step_ref[:, slot, :].astype(bf16))
        fresh = jnp.where(
            is_moved, moved_kv, step_kv_ref[:, slot].reshape(fresh_all, both)
        )
        length = length_ref[me_inst * requests + slot]
        past = lax.dot_general(
            queries, context_ref[:, :head], contract, preferred_element_type=f32
        )
        newer = lax.dot_general(queries, fresh[:, :head], contract, preferred_element_type=f32)
        past = jnp.where((past_head == query_head) & (past_token < length), past, NEG)
        newer = jnp.where(fresh_mask, newer, NEG)
        top = jnp.maximum(
            jnp.max(past, axis=1, keepdims=True), jnp.max(newer, axis=1, keepdims=True)
        )
        past = jnp.exp2((past - top) * factor)
        newer = jnp.exp2((newer - top) * factor)
        total = jnp.sum(past, axis=1, keepdims=True) + jnp.sum(newer, axis=1, keepdims=True)
        share = 1.0 / total
        out = jnp.dot(
            (past * share).astype(bf16), context_ref[:, head:], preferred_element_type=f32
        )
        out = out + jnp.dot(
            (newer * share).astype(bf16), fresh[:, head:], preferred_element_type=f32
        )
        decoded_ref[:, slot, :] = out
        return carry

    lax.fori_loop(0, requests, decode_slot, 0)

    move_o_out[...] = decoded_ref[:, my_slot, :].astype(bf16)
    returns = [move(bit, move_o_out, move_o_in, 2) for bit in range(bits)]
    for copy in returns:
        copy.start()

    size = slots // 2

    def take(part, column, count):
        first = part * (devices // 2)
        rows_in = recv_ref[
            first : first + devices // 2, :, pl.ds(pl.multiple_of(column, 128), count)
        ]
        return rows_in.astype(f32).reshape(size, count).astype(bf16)

    def keys_of(part, h):
        keyvals = take(part, h * unit + group * head, both)
        ones = jnp.ones((size, head), bf16)
        return keyvals[:, :head], jnp.concatenate([keyvals[:, head:], ones], axis=1)

    def attend(part, h, keys, first):
        queries = take(part, h * unit, group * head)
        queries = jnp.concatenate(
            [queries[:, g * head : (g + 1) * head] for g in range(group)], axis=0
        )
        scores = lax.dot_general(queries, keys, contract, preferred_element_type=f32)
        count = keys.shape[0]
        bias = bias_ref[part * size : (part + 1) * size, first : first + count]
        scores = (scores.reshape(group, size, count) + bias[None]).reshape(group * size, count)
        return scores, jnp.max(scores, axis=1, keepdims=True)

    def weigh(scores, top, values):
        expo = jnp.exp2((scores - top) * factor).astype(bf16)
        return jnp.dot(expo, values, preferred_element_type=f32)

    def finish(part, h, out):
        out = out[:, :head] / out[:, head:]
        keep = filled_ref[part * size : (part + 1) * size, :] > 0
        for g in range(group):
            column = pl.multiple_of((h * group + g) * head, 128)
            prefill_ref[part * size : (part + 1) * size, pl.ds(column, head)] = jnp.where(
                keep, out[g * size : (g + 1) * size], 0.0
            ).astype(bf16)

    def lower(h, carry):
        keys, values = keys_of(0, h)
        scores, top = attend(0, h, keys, 0)
        finish(0, h, weigh(scores, top, values))
        return carry

    def upper_alone(h, carry):
        keys, values = keys_of(1, h)
        scores, top = attend(1, h, keys, size)
        part_ref[h] = weigh(scores, top, values)
        part_top_ref[h] = jnp.broadcast_to(top, (group * size, head))
        return carry

    def upper_all(h, carry):
        keys_0, values_0 = keys_of(0, h)
        keys_1, values_1 = keys_of(1, h)
        keys = jnp.concatenate([keys_0, keys_1], axis=0)
        values = jnp.concatenate([values_0, values_1], axis=0)
        scores, top = attend(1, h, keys, 0)
        finish(1, h, weigh(scores, top, values))
        return carry

    def lower_then_upper(h, carry):
        keys, values = keys_of(0, h)
        scores, top = attend(0, h, keys, 0)
        finish(0, h, weigh(scores, top, values))
        scores, top = attend(1, h, keys, 0)
        old_top = part_top_ref[h]
        new_top = jnp.maximum(old_top, top)
        out = weigh(scores, new_top[:, :1], values)
        decay = jnp.exp2((old_top - new_top) * factor)
        out = out + part_ref[h] * jnp.concatenate([decay, decay], axis=1)
        finish(1, h, out)
        return carry

    def loop(body):
        def run():
            lax.fori_loop(0, kv_heads, body, 0)

        return run

    own.wait()
    for j in range(half):
        for t in range(n_tp):
            if j or t:
                inst = near_base + lax.rem(local_inst + j, half)
                source = inst * n_tp + lax.rem(me_tp + t, n_tp)
                shipment(me_inst, me_tp, source).wait_recv()
    pl.when(is_low)(loop(lower))
    pl.when(jnp.logical_not(is_low))(loop(upper_alone))
    for j in range(half):
        for t in range(n_tp):
            inst = far_base + lax.rem(local_inst + j, half)
            source = inst * n_tp + lax.rem(me_tp + t, n_tp)
            shipment(me_inst, me_tp, source).wait_recv()
    pl.when(is_low)(loop(upper_all))
    pl.when(jnp.logical_not(is_low))(loop(lower_then_upper))

    for copy in returns:
        copy.wait()
    moved_o = move_o_in[0].astype(f32)
    for bit in range(1, bits):
        match = (distance == (1 << bit)) | (distance == -(1 << bit))
        moved_o = jnp.where(match, move_o_in[bit].astype(f32), moved_o)
    slot_row = lax.broadcasted_iota(jnp.int32, (requests, 1), 0)
    for t in range(steps):
        for h in range(heads):
            row = t * heads + h
            decode_ref[t, :, h * head : (h + 1) * head] = jnp.where(
                slot_row == my_slot, moved_o[row : row + 1, :], decoded_ref[row]
            ).astype(bf16)

    for j in range(n_inst):
        for t in range(n_tp):
            if j or t:
                inst, tp = lax.rem(me_inst + j, n_inst), lax.rem(me_tp + t, n_tp)
                shipment(inst, tp, me).wait_send()


def local_fused(
    step_queries,
    step_keyvals,
    cache_pages,
    block_table,
    context_len,
    partner,
    moved_slot,
    prompt_queries,
    prompt_keyvals,
    prompt_target,
):
    n_inst, n_tp = lax.axis_size("inst"), lax.axis_size("tp")
    devices = n_inst * n_tp
    bits = n_inst.bit_length() - 1
    steps, requests, width = step_queries.shape
    kv_heads, both = step_keyvals.shape[2:]
    head = both // 2
    heads = width // head
    cap = 2 * prompt_queries.shape[0] // n_inst
    slots = devices * cap
    columns = width + kv_heads * both
    span = block_table.shape[1] * cache_pages.shape[1] * kv_heads
    bf16, f32 = jnp.bfloat16, jnp.float32
    smem = pl.BlockSpec(memory_space=pltpu.SMEM)
    vmem = pl.BlockSpec(memory_space=pltpu.VMEM)
    hbm = pl.BlockSpec(memory_space=pltpu.HBM)
    return pl.pallas_call(
        functools.partial(fused_kernel, n_inst, n_tp),
        out_shape=(
            pltpu.VMEM(step_queries.shape, bf16),
            pltpu.VMEM((slots, width), bf16),
        ),
        in_specs=[smem] * 4
        + [hbm] * 5 + [vmem],
        out_specs=(vmem, vmem),
        scratch_shapes=[
            pltpu.VMEM(cache_pages.shape, bf16),
            pltpu.VMEM(step_queries.shape, bf16),
            pltpu.VMEM(step_keyvals.shape, bf16),
            pltpu.VMEM((n_tp, prompt_queries.shape[0], width), bf16),
            pltpu.VMEM(prompt_keyvals.shape, bf16),
            pltpu.VMEM((n_tp, n_inst, cap, columns), bf16),
            pltpu.VMEM((devices, cap, columns), bf16),
            pltpu.VMEM((steps * heads, requests, head), f32),
            pltpu.VMEM((span, both), bf16),
            pltpu.VMEM((steps * heads, requests, head), f32),
            pltpu.VMEM((steps * heads, head), bf16),
            pltpu.VMEM((steps * kv_heads, both), bf16),
            pltpu.VMEM((bits, steps * heads, head), bf16),
            pltpu.VMEM((bits, steps * kv_heads, both), bf16),
            pltpu.VMEM((steps * heads, head), bf16),
            pltpu.VMEM((bits, steps * heads, head), bf16),
            pltpu.VMEM((slots, slots), f32),
            pltpu.VMEM((slots, head), f32),
            pltpu.VMEM((kv_heads, heads // kv_heads * slots // 2, both), f32),
            pltpu.VMEM((kv_heads, heads // kv_heads * slots // 2, head), f32),
            pltpu.SemaphoreType.DMA,
            pltpu.SemaphoreType.DMA((3,)),
            pltpu.SemaphoreType.DMA((n_tp,)),
            pltpu.SemaphoreType.DMA,
            pltpu.SemaphoreType.DMA((devices,)),
            pltpu.SemaphoreType.DMA((devices,)),
            pltpu.SemaphoreType.DMA((3, bits)),
            pltpu.SemaphoreType.DMA((3, bits)),
        ],
        compiler_params=pltpu.CompilerParams(
            collective_id=0, has_side_effects=True, vmem_limit_bytes=58 << 20
        ),
    )(
        block_table,
        context_len,
        partner,
        moved_slot,
        step_queries,
        step_keyvals,
        cache_pages,
        prompt_queries,
        prompt_keyvals,
        prompt_target.reshape(n_inst, -1),
    )


def local_plain(
    step_queries,
    step_keyvals,
    cache_pages,
    block_table,
    context_len,
    partner,
    moved_slot,
    prompt_queries,
    prompt_keyvals,
    prompt_target,
):
    inst_count = lax.axis_size("inst")
    tp_count = lax.axis_size("tp")
    me_inst = lax.axis_index("inst")
    me_tp = lax.axis_index("tp")
    requests = block_table.shape[0]
    kv_heads = step_keyvals.shape[2]
    head_dim = step_keyvals.shape[3] // 2
    rows_dev = prompt_queries.shape[0]
    capacity = max(2, 2 * rows_dev // inst_count)
    devices = inst_count * tp_count
    targets = prompt_target[:, 0].reshape(devices, rows_dev)
    mine = lax.dynamic_index_in_dim(targets, me_inst * tp_count + me_tp, 0, keepdims=False)
    onehot = (mine[:, None] == jnp.arange(inst_count, dtype=jnp.int32)[None, :]).astype(jnp.int32)
    rank = jnp.sum((jnp.cumsum(onehot, axis=0) - onehot) * onehot, axis=1)
    place = mine * capacity + rank
    dispatch = (
        jnp.arange(inst_count * capacity, dtype=jnp.int32)[:, None] == place[None, :]
    ).astype(jnp.bfloat16)
    send_queries = (
        jnp.dot(dispatch, prompt_queries, preferred_element_type=jnp.float32)
        .astype(jnp.bfloat16)
        .reshape(inst_count, capacity, -1)
    )
    flat_keyvals = prompt_keyvals.reshape(rows_dev, -1)
    send_keyvals = (
        jnp.dot(dispatch, flat_keyvals, preferred_element_type=jnp.float32)
        .astype(jnp.bfloat16)
        .reshape(inst_count, capacity, -1)
    )
    recv_queries, recv_keyvals = (
        lax.all_to_all(
            lax.all_to_all(send_queries, "inst", split_axis=0, concat_axis=0, tiled=True),
            "tp",
            split_axis=2,
            concat_axis=1,
            tiled=True,
        ),
        lax.all_to_all(
            lax.all_to_all(send_keyvals, "inst", split_axis=0, concat_axis=0, tiled=True),
            "tp",
            split_axis=2,
            concat_axis=1,
            tiled=True,
        ),
    )
    gathered = cache_pages[block_table]
    context = gathered.reshape(requests, -1, kv_heads, 2 * head_dim)
    lengths = lax.dynamic_slice_in_dim(context_len, me_inst * requests, requests)
    my_slot = moved_slot[me_inst]
    other = partner[me_inst]
    other_len = context_len[other * requests + moved_slot[other]]
    bit_total = inst_count.bit_length() - 1
    distance = jnp.bitwise_xor(me_inst, other)
    outgoing = lax.dynamic_index_in_dim(context, my_slot, 0, keepdims=False)
    incoming = outgoing
    for bit in range(bit_total):
        arrived = swapped(outgoing, "inst", bit)
        incoming = jnp.where(distance == 1 << bit, arrived, incoming)
    context = lax.dynamic_update_index_in_dim(context, incoming, my_slot, 0)
    lengths = lengths.at[my_slot].set(other_len)
    decode_output = decode_block(step_queries, context, lengths, step_keyvals)
    slots = inst_count * tp_count * capacity
    slot_queries = recv_queries.reshape(slots, -1)
    slot_keyvals = recv_keyvals.reshape(slots, kv_heads, 2 * head_dim)
    counts = jnp.sum((targets == me_inst).astype(jnp.int32), axis=1)
    valid = (jnp.arange(capacity, dtype=jnp.int32)[None, :] < counts[:, None]).reshape(slots)
    prefill_output = prefill_block(slot_queries, slot_keyvals, valid)
    return (decode_output, prefill_output)


def local(*arrays):
    rows_dev = arrays[7].shape[0]
    if (2 * rows_dev // lax.axis_size("inst")) % 8:
        return local_plain(*arrays)
    return local_fused(*arrays)


def solution(mesh):
    placed = (
        P(None, "inst", "tp"),
        P(None, "inst", "tp", None),
        P("inst", None, "tp", None),
        P("inst", None),
        P(),
        P(),
        P(),
        P(("inst", "tp"), None),
        P(("inst", "tp"), None, None),
        P(),
    )
    return jax.shard_map(
        local,
        mesh=mesh,
        in_specs=placed,
        out_specs=(P(None, "inst", "tp"), P("inst", "tp")),
        check_vma=False,
    )
```

```python
import functools
import math

import jax
import jax.numpy as jnp
from jax import lax
from jax.experimental import pallas as pl
from jax.experimental.pallas import tpu as pltpu
from jax.sharding import PartitionSpec as P


def swapped(array, axis, bit):
    return lax.ppermute(array, axis, [(i, i ^ 1 << bit) for i in range(lax.axis_size(axis))])


def masked_weights(scores, mask):
    shifted = jnp.where(mask, scores, jnp.float32(-1e30))
    top = jnp.max(shifted, axis=-1, keepdims=True)
    expo = jnp.where(mask, jnp.exp(shifted - top), jnp.float32(0.0))
    total = jnp.sum(expo, axis=-1, keepdims=True)
    total = jnp.where(total > 0, total, jnp.float32(1.0))
    return expo / total


def decode_block(queries, context, lengths, fresh):
    steps, count, width = queries.shape
    kv_heads = context.shape[2]
    head_dim = context.shape[3] // 2
    group = width // (kv_heads * head_dim)
    span = context.shape[1]
    scale = head_dim ** (-0.5)
    query = queries.reshape(steps, count, kv_heads, group, head_dim)
    past = (
        jnp.einsum(
            "trkgd,rckd->trkgc", query, context[..., :head_dim], preferred_element_type=jnp.float32
        )
        * scale
    )
    newer = (
        jnp.einsum(
            "trkgd,urkd->trkgu", query, fresh[..., :head_dim], preferred_element_type=jnp.float32
        )
        * scale
    )
    past_mask = (jnp.arange(span, dtype=jnp.int32)[None, :] < lengths[:, None])[
        None, :, None, None, :
    ]
    step_ids = jnp.arange(steps, dtype=jnp.int32)
    new_mask = (step_ids[None, :] <= step_ids[:, None])[:, None, None, None, :]
    mask = jnp.concatenate(
        [jnp.broadcast_to(past_mask, past.shape), jnp.broadcast_to(new_mask, newer.shape)], axis=-1
    )
    weights = masked_weights(jnp.concatenate([past, newer], axis=-1), mask).astype(jnp.bfloat16)
    out = jnp.einsum(
        "trkgc,rckd->trkgd",
        weights[..., :span],
        context[..., head_dim:],
        preferred_element_type=jnp.float32,
    )
    out = out + jnp.einsum(
        "trkgu,urkd->trkgd",
        weights[..., span:],
        fresh[..., head_dim:],
        preferred_element_type=jnp.float32,
    )
    return out.reshape(steps, count, width).astype(jnp.bfloat16)


def prefill_block(queries, keyvals, valid):
    slots, width = queries.shape
    kv_heads = keyvals.shape[1]
    head_dim = keyvals.shape[2] // 2
    group = width // (kv_heads * head_dim)
    scale = head_dim ** (-0.5)
    query = queries.reshape(slots, kv_heads, group, head_dim)
    block = 512 if slots % 512 == 0 else slots
    pieces = []
    for start in range(0, slots, block):
        finish = start + block
        scores = (
            jnp.einsum(
                "qkgd,ckd->kgqc",
                query[start:finish],
                keyvals[:finish, :, :head_dim],
                preferred_element_type=jnp.float32,
            )
            * scale
        )
        query_pos = jnp.arange(start, finish, dtype=jnp.int32)
        key_pos = jnp.arange(finish, dtype=jnp.int32)
        mask = (valid[None, :finish] & (key_pos[None, :] <= query_pos[:, None]))[None, None]
        weights = masked_weights(scores, jnp.broadcast_to(mask, scores.shape)).astype(jnp.bfloat16)
        out = jnp.einsum(
            "kgqc,ckd->qkgd",
            weights,
            keyvals[:finish, :, head_dim:],
            preferred_element_type=jnp.float32,
        )
        out = jnp.where(valid[start:finish, None, None, None], out, jnp.float32(0.0))
        pieces.append(out.reshape(block, width).astype(jnp.bfloat16))
    return jnp.concatenate(pieces, axis=0)


MESH = pl.DeviceIdType.MESH
NEG = -1e30


def fused_kernel(
    n_inst,
    n_tp,
    block_ref,
    length_ref,
    partner_ref,
    moved_ref,
    step_q_hbm,
    step_kv_hbm,
    cache_hbm,
    prompt_q_hbm,
    prompt_kv_hbm,
    target_ref,
    decode_ref,
    prefill_ref,
    cache_ref,
    step_q_ref,
    step_kv_ref,
    prompt_q_ref,
    prompt_kv_ref,
    send_ref,
    recv_ref,
    step_ref,
    context_ref,
    decoded_ref,
    move_q_out,
    move_kv_out,
    move_q_in,
    move_kv_in,
    move_o_out,
    move_o_in,
    bias_ref,
    filled_ref,
    part_ref,
    part_top_ref,
    cache_sem,
    small_sem,
    prompt_sem,
    self_sem,
    send_sem,
    recv_sem,
    move_send_sem,
    move_recv_sem,
):
    f32, bf16 = jnp.float32, jnp.bfloat16
    me_inst, me_tp = lax.axis_index("inst"), lax.axis_index("tp")
    me = me_inst * n_tp + me_tp
    devices = n_inst * n_tp
    bits = n_inst.bit_length() - 1
    steps, requests, width = step_q_hbm.shape
    kv_heads, both = step_kv_ref.shape[2:]
    head = both // 2
    heads = width // head
    group = heads // kv_heads
    rows = prompt_q_ref.shape[1]
    cap = recv_ref.shape[1]
    slots = devices * cap
    pages, page = block_ref.shape[1], cache_ref.shape[1]
    unit = group * head + both
    factor = head**-0.5 * math.log2(math.e)

    tps = [lax.rem(me_tp + t, n_tp) for t in range(n_tp)]
    prompt_copies = [
        pltpu.make_async_copy(
            prompt_q_hbm.at[:, pl.ds(pl.multiple_of(tps[t] * width, 128), width)],
            prompt_q_ref.at[t],
            prompt_sem.at[t],
        )
        for t in range(n_tp)
    ]
    small_copies = [
        pltpu.make_async_copy(source, target, small_sem.at[i])
        for i, (source, target) in enumerate(
            [
                (prompt_kv_hbm, prompt_kv_ref),
                (step_q_hbm, step_q_ref),
                (step_kv_hbm, step_kv_ref),
            ]
        )
    ]
    small_copies[0].start()
    for copy in prompt_copies:
        copy.start()
    for copy in small_copies[1:]:
        copy.start()
    cache_copy = pltpu.make_async_copy(cache_hbm, cache_ref, cache_sem)
    cache_copy.start()

    barrier = pltpu.get_barrier_semaphore()
    for turn in range(1, devices):
        inst = lax.rem(me_inst + turn // n_tp, n_inst)
        tp = lax.rem(me_tp + turn % n_tp, n_tp)
        pl.semaphore_signal(barrier, inc=1, device_id=(inst, tp), device_id_type=MESH)

    lanes = n_tp * rows
    mine = target_ref[pl.ds(me_inst, 1), :]
    onehot = (lax.broadcasted_iota(jnp.int32, (n_inst, lanes), 0) == mine).astype(f32)
    row_from = lax.broadcasted_iota(jnp.int32, (lanes, lanes), 0)
    row_to = lax.broadcasted_iota(jnp.int32, (lanes, lanes), 1)
    earlier = ((row_from < row_to) & (row_from // rows == row_to // rows)).astype(bf16)
    before = jnp.dot(onehot.astype(bf16), earlier, preferred_element_type=f32)
    rank = jnp.sum(before * onehot, axis=0, keepdims=True)
    place = mine.astype(f32) * cap + rank
    both_rows = (
        lax.broadcasted_iota(jnp.int32, (n_inst * cap, lanes), 0).astype(f32) == place
    ).astype(f32)
    dispatch = both_rows[:, :rows]
    for tp in range(1, n_tp):
        dispatch = jnp.where(me_tp == tp, both_rows[:, tp * rows : (tp + 1) * rows], dispatch)

    half = n_inst // 2
    local_inst = lax.rem(me_inst, half)
    near_base = me_inst - local_inst
    far_base = half - near_base
    is_low = me_inst < half
    low, high = dispatch[: half * cap], dispatch[half * cap :]
    far_rows = jnp.where(is_low, high, low).astype(bf16)
    near_rows = jnp.where(is_low, low, high).astype(bf16)

    def pack(t, base, chosen):
        insts = pl.ds(base, half)
        for h in range(kv_heads):
            start = h * group * head
            queries = prompt_q_ref[t, :, start : start + group * head]
            packed = jnp.dot(chosen, queries, preferred_element_type=f32)
            send_ref[tps[t], insts, :, h * unit : h * unit + group * head] = packed.reshape(
                half, cap, group * head
            ).astype(bf16)
            keyvals = prompt_kv_ref[:, h, :]
            for tp in range(1, n_tp):
                keyvals = jnp.where(
                    tps[t] == tp, prompt_kv_ref[:, tp * kv_heads + h, :], keyvals
                )
            packed = jnp.dot(chosen, keyvals, preferred_element_type=f32)
            send_ref[tps[t], insts, :, h * unit + group * head : (h + 1) * unit] = (
                packed.reshape(half, cap, both).astype(bf16)
            )

    my_slot = moved_ref[me_inst]
    distance = partner_ref[me_inst] - me_inst

    def prepare_moves():
        for copy in small_copies[1:]:
            copy.wait()
        for t in range(steps):
            for h in range(heads):
                step_ref[t * heads + h] = step_q_ref[t, :, h * head : (h + 1) * head].astype(f32)
        move_q_out[...] = step_ref[:, my_slot, :].astype(bf16)
        move_kv_out[...] = step_kv_ref[:, my_slot].reshape(steps * kv_heads, both)

    def neighbour(bit):
        return me_inst + (1 - 2 * lax.rem(me_inst // (1 << bit), 2)) * (1 << bit)

    def move(bit, source, target, which):
        return pltpu.make_async_remote_copy(
            src_ref=source,
            dst_ref=target.at[bit],
            send_sem=move_send_sem.at[which, bit],
            recv_sem=move_recv_sem.at[which, bit],
            device_id=(neighbour(bit), me_tp),
            device_id_type=MESH,
        )

    moves = []
    for bit in range(bits):
        moves.append(move(bit, move_q_out, move_q_in, 0))
        moves.append(move(bit, move_kv_out, move_kv_in, 1))

    def shipment(inst, tp, source):
        return pltpu.make_async_remote_copy(
            src_ref=send_ref.at[tp, inst],
            dst_ref=recv_ref.at[source],
            send_sem=send_sem.at[inst * n_tp + tp],
            recv_sem=recv_sem.at[source],
            device_id=(inst, tp),
            device_id_type=MESH,
        )

    def send(base, t, j):
        if base is far_base or j or t:
            shipment(base + lax.rem(local_inst + j, half), tps[t], me).start()

    small_copies[0].wait()
    far, near = [], []
    for t in range(n_tp):
        prompt_copies[t].wait()
        pack(t, far_base, far_rows)
        far.extend((t, j) for j in range(half))
        if t == 0:
            pl.semaphore_wait(barrier, devices - 1)
            send(far_base, *far.pop(0))
            send(far_base, *far.pop(0))
            prepare_moves()
            for copy in moves:
                copy.start()
        pack(t, near_base, near_rows)
        near.extend((t, j) for j in range(half))
        while far:
            for _ in range(-(-len(near) // len(far)) if t == n_tp - 1 else 1):
                if near:
                    send(near_base, *near.pop(0))
            send(far_base, *far.pop(0))
    for entry in near:
        send(near_base, *entry)
    own = pltpu.make_async_copy(send_ref.at[me_tp, me_inst], recv_ref.at[me], self_sem)
    own.start()

    here = (target_ref[...] == me_inst).astype(bf16)
    slot = lax.broadcasted_iota(jnp.int32, (slots, 1), 0)
    spread = (
        slot // (n_tp * cap) == lax.broadcasted_iota(jnp.int32, (slots, n_inst), 1)
    ).astype(bf16)
    named = jnp.dot(spread, here, preferred_element_type=f32)
    lane = lax.broadcasted_iota(jnp.int32, (slots, lanes), 1)
    named = jnp.where(lane // rows == lax.rem(slot // cap, n_tp), named, 0.0)
    counts = jnp.sum(named, axis=1, keepdims=True)
    filled = (lax.rem(slot, cap).astype(f32) < counts).astype(f32)
    filled = jnp.broadcast_to(filled, (slots, head))
    filled_ref[...] = filled
    across = jnp.transpose(filled)[0:1, :]
    query_pos = lax.broadcasted_iota(jnp.int32, (slots, slots), 0)
    key_pos = lax.broadcasted_iota(jnp.int32, (slots, slots), 1)
    bias_ref[...] = jnp.where((key_pos <= query_pos) & (across > 0), 0.0, NEG)

    cache_copy.wait()
    for copy in moves:
        copy.wait()
    moved_q, moved_kv = move_q_in[0].astype(f32), move_kv_in[0].astype(f32)
    for bit in range(1, bits):
        match = (distance == (1 << bit)) | (distance == -(1 << bit))
        moved_q = jnp.where(match, move_q_in[bit].astype(f32), moved_q)
        moved_kv = jnp.where(match, move_kv_in[bit].astype(f32), moved_kv)
    moved_q, moved_kv = moved_q.astype(bf16), moved_kv.astype(bf16)

    queries_all = steps * heads
    span = pages * page * kv_heads
    fresh_all = steps * kv_heads
    query_row = lax.broadcasted_iota(jnp.int32, (queries_all, 1), 0)
    query_head = lax.rem(query_row, heads) // group
    query_step = query_row // heads
    past_col = lax.broadcasted_iota(jnp.int32, (1, span), 1)
    past_head = lax.rem(past_col, kv_heads)
    page_row = lax.rem(past_col, page * kv_heads)
    past_token = (
        past_col // (page * kv_heads) * page
        + page_row // (2 * kv_heads)
        + lax.rem(page_row // kv_heads, 2) * (page // 2)
    )
    fresh_col = lax.broadcasted_iota(jnp.int32, (1, fresh_all), 1)
    fresh_mask = (lax.rem(fresh_col, kv_heads) == query_head) & (
        fresh_col // kv_heads <= query_step
    )
    contract = (((1,), (1,)), ((), ()))

    def decode_slot(slot, carry):
        for i in range(pages):
            tokens = cache_ref[block_ref[slot, i]].astype(f32)
            paired = jnp.concatenate([tokens[: page // 2], tokens[page // 2 :]], axis=1)
            context_ref[i * page * kv_heads : (i + 1) * page * kv_heads, :] = paired.reshape(
                page * kv_heads, both
            ).astype(bf16)
        is_moved = slot == my_slot
        queries = jnp.where(is_moved, moved_q, step_ref[:, slot, :].astype(bf16))
        fresh = jnp.where(
            is_moved, moved_kv, step_kv_ref[:, slot].reshape(fresh_all, both)
        )
        length = length_ref[me_inst * requests + slot]
        past = lax.dot_general(
            queries, context_ref[:, :head], contract, preferred_element_type=f32
        )
        newer = lax.dot_general(queries, fresh[:, :head], contract, preferred_element_type=f32)
        past = jnp.where((past_head == query_head) & (past_token < length), past, NEG)
        newer = jnp.where(fresh_mask, newer, NEG)
        top = jnp.maximum(
            jnp.max(past, axis=1, keepdims=True), jnp.max(newer, axis=1, keepdims=True)
        )
        past = jnp.exp2((past - top) * factor)
        newer = jnp.exp2((newer - top) * factor)
        total = jnp.sum(past, axis=1, keepdims=True) + jnp.sum(newer, axis=1, keepdims=True)
        share = 1.0 / total
        out = jnp.dot(
            (past * share).astype(bf16), context_ref[:, head:], preferred_element_type=f32
        )
        out = out + jnp.dot(
            (newer * share).astype(bf16), fresh[:, head:], preferred_element_type=f32
        )
        decoded_ref[:, slot, :] = out
        return carry

    lax.fori_loop(0, requests, decode_slot, 0)

    move_o_out[...] = decoded_ref[:, my_slot, :].astype(bf16)
    returns = [move(bit, move_o_out, move_o_in, 2) for bit in range(bits)]
    for copy in returns:
        copy.start()

    size = slots // 2

    def take(part, column, count):
        first = part * (devices // 2)
        rows_in = recv_ref[
            first : first + devices // 2, :, pl.ds(pl.multiple_of(column, 128), count)
        ]
        return rows_in.astype(f32).reshape(size, count).astype(bf16)

    def keys_of(part, h):
        keyvals = take(part, h * unit + group * head, both)
        ones = jnp.ones((size, head), bf16)
        return keyvals[:, :head], jnp.concatenate([keyvals[:, head:], ones], axis=1)

    def attend(part, h, keys, first):
        queries = take(part, h * unit, group * head)
        queries = jnp.concatenate(
            [queries[:, g * head : (g + 1) * head] for g in range(group)], axis=0
        )
        scores = lax.dot_general(queries, keys, contract, preferred_element_type=f32)
        count = keys.shape[0]
        bias = bias_ref[part * size : (part + 1) * size, first : first + count]
        scores = (scores.reshape(group, size, count) + bias[None]).reshape(group * size, count)
        return scores, jnp.max(scores, axis=1, keepdims=True)

    def weigh(scores, top, values):
        expo = jnp.exp2((scores - top) * factor).astype(bf16)
        return jnp.dot(expo, values, preferred_element_type=f32)

    def finish(part, h, out):
        out = out[:, :head] / out[:, head:]
        keep = filled_ref[part * size : (part + 1) * size, :] > 0
        for g in range(group):
            column = pl.multiple_of((h * group + g) * head, 128)
            prefill_ref[part * size : (part + 1) * size, pl.ds(column, head)] = jnp.where(
                keep, out[g * size : (g + 1) * size], 0.0
            ).astype(bf16)

    def lower(h, carry):
        keys, values = keys_of(0, h)
        scores, top = attend(0, h, keys, 0)
        finish(0, h, weigh(scores, top, values))
        return carry

    def upper_alone(h, carry):
        keys, values = keys_of(1, h)
        scores, top = attend(1, h, keys, size)
        part_ref[h] = weigh(scores, top, values)
        part_top_ref[h] = jnp.broadcast_to(top, (group * size, head))
        return carry

    def upper_all(h, carry):
        keys_0, values_0 = keys_of(0, h)
        keys_1, values_1 = keys_of(1, h)
        keys = jnp.concatenate([keys_0, keys_1], axis=0)
        values = jnp.concatenate([values_0, values_1], axis=0)
        scores, top = attend(1, h, keys, 0)
        finish(1, h, weigh(scores, top, values))
        return carry

    def lower_then_upper(h, carry):
        keys, values = keys_of(0, h)
        scores, top = attend(0, h, keys, 0)
        finish(0, h, weigh(scores, top, values))
        scores, top = attend(1, h, keys, 0)
        old_top = part_top_ref[h]
        new_top = jnp.maximum(old_top, top)
        out = weigh(scores, new_top[:, :1], values)
        decay = jnp.exp2((old_top - new_top) * factor)
        out = out + part_ref[h] * jnp.concatenate([decay, decay], axis=1)
        finish(1, h, out)
        return carry

    def loop(body):
        def run():
            lax.fori_loop(0, kv_heads, body, 0)

        return run

    own.wait()
    for j in range(half):
        for t in range(n_tp):
            if j or t:
                inst = near_base + lax.rem(local_inst + j, half)
                source = inst * n_tp + lax.rem(me_tp + t, n_tp)
                shipment(me_inst, me_tp, source).wait_recv()
    pl.when(is_low)(loop(lower))
    pl.when(jnp.logical_not(is_low))(loop(upper_alone))
    for j in range(half):
        for t in range(n_tp):
            inst = far_base + lax.rem(local_inst + j, half)
            source = inst * n_tp + lax.rem(me_tp + t, n_tp)
            shipment(me_inst, me_tp, source).wait_recv()
    pl.when(is_low)(loop(upper_all))
    pl.when(jnp.logical_not(is_low))(loop(lower_then_upper))

    for copy in returns:
        copy.wait()
    moved_o = move_o_in[0].astype(f32)
    for bit in range(1, bits):
        match = (distance == (1 << bit)) | (distance == -(1 << bit))
        moved_o = jnp.where(match, move_o_in[bit].astype(f32), moved_o)
    slot_row = lax.broadcasted_iota(jnp.int32, (requests, 1), 0)
    for t in range(steps):
        for h in range(heads):
            row = t * heads + h
            decode_ref[t, :, h * head : (h + 1) * head] = jnp.where(
                slot_row == my_slot, moved_o[row : row + 1, :], decoded_ref[row]
            ).astype(bf16)

    for j in range(n_inst):
        for t in range(n_tp):
            if j or t:
                inst, tp = lax.rem(me_inst + j, n_inst), lax.rem(me_tp + t, n_tp)
                shipment(inst, tp, me).wait_send()


def local_fused(
    step_queries,
    step_keyvals,
    cache_pages,
    block_table,
    context_len,
    partner,
    moved_slot,
    prompt_queries,
    prompt_keyvals,
    prompt_target,
):
    n_inst, n_tp = lax.axis_size("inst"), lax.axis_size("tp")
    devices = n_inst * n_tp
    bits = n_inst.bit_length() - 1
    steps, requests, width = step_queries.shape
    kv_heads, both = step_keyvals.shape[2:]
    head = both // 2
    heads = width // head
    cap = 2 * prompt_queries.shape[0] // n_inst
    slots = devices * cap
    columns = width + kv_heads * both
    span = block_table.shape[1] * cache_pages.shape[1] * kv_heads
    bf16, f32 = jnp.bfloat16, jnp.float32
    smem = pl.BlockSpec(memory_space=pltpu.SMEM)
    vmem = pl.BlockSpec(memory_space=pltpu.VMEM)
    hbm = pl.BlockSpec(memory_space=pltpu.HBM)
    return pl.pallas_call(
        functools.partial(fused_kernel, n_inst, n_tp),
        out_shape=(
            pltpu.VMEM(step_queries.shape, bf16),
            pltpu.VMEM((slots, width), bf16),
        ),
        in_specs=[smem] * 4
        + [hbm] * 5 + [vmem],
        out_specs=(vmem, vmem),
        scratch_shapes=[
            pltpu.VMEM(cache_pages.shape, bf16),
            pltpu.VMEM(step_queries.shape, bf16),
            pltpu.VMEM(step_keyvals.shape, bf16),
            pltpu.VMEM((n_tp, prompt_queries.shape[0], width), bf16),
            pltpu.VMEM(prompt_keyvals.shape, bf16),
            pltpu.VMEM((n_tp, n_inst, cap, columns), bf16),
            pltpu.VMEM((devices, cap, columns), bf16),
            pltpu.VMEM((steps * heads, requests, head), f32),
            pltpu.VMEM((span, both), bf16),
            pltpu.VMEM((steps * heads, requests, head), f32),
            pltpu.VMEM((steps * heads, head), bf16),
            pltpu.VMEM((steps * kv_heads, both), bf16),
            pltpu.VMEM((bits, steps * heads, head), bf16),
            pltpu.VMEM((bits, steps * kv_heads, both), bf16),
            pltpu.VMEM((steps * heads, head), bf16),
            pltpu.VMEM((bits, steps * heads, head), bf16),
            pltpu.VMEM((slots, slots), f32),
            pltpu.VMEM((slots, head), f32),
            pltpu.VMEM((kv_heads, heads // kv_heads * slots // 2, both), f32),
            pltpu.VMEM((kv_heads, heads // kv_heads * slots // 2, head), f32),
            pltpu.SemaphoreType.DMA,
            pltpu.SemaphoreType.DMA((3,)),
            pltpu.SemaphoreType.DMA((n_tp,)),
            pltpu.SemaphoreType.DMA,
            pltpu.SemaphoreType.DMA((devices,)),
            pltpu.SemaphoreType.DMA((devices,)),
            pltpu.SemaphoreType.DMA((3, bits)),
            pltpu.SemaphoreType.DMA((3, bits)),
        ],
        compiler_params=pltpu.CompilerParams(
            collective_id=0, has_side_effects=True, vmem_limit_bytes=58 << 20
        ),
    )(
        block_table,
        context_len,
        partner,
        moved_slot,
        step_queries,
        step_keyvals,
        cache_pages,
        prompt_queries,
        prompt_keyvals,
        prompt_target.reshape(n_inst, -1),
    )


def local_plain(
    step_queries,
    step_keyvals,
    cache_pages,
    block_table,
    context_len,
    partner,
    moved_slot,
    prompt_queries,
    prompt_keyvals,
    prompt_target,
):
    inst_count = lax.axis_size("inst")
    tp_count = lax.axis_size("tp")
    me_inst = lax.axis_index("inst")
    me_tp = lax.axis_index("tp")
    requests = block_table.shape[0]
    kv_heads = step_keyvals.shape[2]
    head_dim = step_keyvals.shape[3] // 2
    rows_dev = prompt_queries.shape[0]
    capacity = max(2, 2 * rows_dev // inst_count)
    devices = inst_count * tp_count
    targets = prompt_target[:, 0].reshape(devices, rows_dev)
    mine = lax.dynamic_index_in_dim(targets, me_inst * tp_count + me_tp, 0, keepdims=False)
    onehot = (mine[:, None] == jnp.arange(inst_count, dtype=jnp.int32)[None, :]).astype(jnp.int32)
    rank = jnp.sum((jnp.cumsum(onehot, axis=0) - onehot) * onehot, axis=1)
    place = mine * capacity + rank
    dispatch = (
        jnp.arange(inst_count * capacity, dtype=jnp.int32)[:, None] == place[None, :]
    ).astype(jnp.bfloat16)
    send_queries = (
        jnp.dot(dispatch, prompt_queries, preferred_element_type=jnp.float32)
        .astype(jnp.bfloat16)
        .reshape(inst_count, capacity, -1)
    )
    flat_keyvals = prompt_keyvals.reshape(rows_dev, -1)
    send_keyvals = (
        jnp.dot(dispatch, flat_keyvals, preferred_element_type=jnp.float32)
        .astype(jnp.bfloat16)
        .reshape(inst_count, capacity, -1)
    )
    recv_queries, recv_keyvals = (
        lax.all_to_all(
            lax.all_to_all(send_queries, "inst", split_axis=0, concat_axis=0, tiled=True),
            "tp",
            split_axis=2,
            concat_axis=1,
            tiled=True,
        ),
        lax.all_to_all(
            lax.all_to_all(send_keyvals, "inst", split_axis=0, concat_axis=0, tiled=True),
            "tp",
            split_axis=2,
            concat_axis=1,
            tiled=True,
        ),
    )
    gathered = cache_pages[block_table]
    context = gathered.reshape(requests, -1, kv_heads, 2 * head_dim)
    lengths = lax.dynamic_slice_in_dim(context_len, me_inst * requests, requests)
    my_slot = moved_slot[me_inst]
    other = partner[me_inst]
    other_len = context_len[other * requests + moved_slot[other]]
    bit_total = inst_count.bit_length() - 1
    distance = jnp.bitwise_xor(me_inst, other)
    outgoing = lax.dynamic_index_in_dim(context, my_slot, 0, keepdims=False)
    incoming = outgoing
    for bit in range(bit_total):
        arrived = swapped(outgoing, "inst", bit)
        incoming = jnp.where(distance == 1 << bit, arrived, incoming)
    context = lax.dynamic_update_index_in_dim(context, incoming, my_slot, 0)
    lengths = lengths.at[my_slot].set(other_len)
    decode_output = decode_block(step_queries, context, lengths, step_keyvals)
    slots = inst_count * tp_count * capacity
    slot_queries = recv_queries.reshape(slots, -1)
    slot_keyvals = recv_keyvals.reshape(slots, kv_heads, 2 * head_dim)
    counts = jnp.sum((targets == me_inst).astype(jnp.int32), axis=1)
    valid = (jnp.arange(capacity, dtype=jnp.int32)[None, :] < counts[:, None]).reshape(slots)
    prefill_output = prefill_block(slot_queries, slot_keyvals, valid)
    return (decode_output, prefill_output)


def local(*arrays):
    rows_dev = arrays[7].shape[0]
    if (2 * rows_dev // lax.axis_size("inst")) % 8:
        return local_plain(*arrays)
    return local_fused(*arrays)


def solution(mesh):
    placed = (
        P(None, "inst", "tp"),
        P(None, "inst", "tp", None),
        P("inst", None, "tp", None),
        P("inst", None),
        P(),
        P(),
        P(),
        P(("inst", "tp"), None),
        P(("inst", "tp"), None, None),
        P(),
    )
    return jax.shard_map(
        local,
        mesh=mesh,
        in_specs=placed,
        out_specs=(P(None, "inst", "tp"), P("inst", "tp")),
        check_vma=False,
    )
```
